32 devices in a mesh: cand: 2 (over x), tp: 4 (over z), dp: 4 (over y, core).
Axes of the slice: x: 2, y: 2, z: 4, core: 2. Of those that a mesh axis runs over, the one named last changes fastest.
Arguments:
- tokens: bfloat16 [4, 4, 256, 4096], P('dp', 'cand')
- qkv_weight: bfloat16 [4096, 4, 768], P(None, 'tp'), may hold values from -0.09375 to 0.09375
- lengths: int32 [4, 4], P('dp', 'cand'), may hold values from 64 to 256, as said below
- grad_out: bfloat16 [4, 4, 256, 4, 512], P('dp', 'cand', None, 'tp')
Outputs:
- attended: bfloat16 [4, 4, 256, 4, 512], P('dp', 'cand', None, 'tp')
- grad_x: bfloat16 [4, 4, 256, 4096], P('dp', 'cand', None, 'tp')
- grad_w: float32 [4096, 4, 768], P(('cand', 'dp'), 'tp')
The draws below stay inside these ranges and needn't reach their ends.
Inputs may be any that keep to these rules, and one draw needn't show every extreme that they name: `lengths`: some passage in each draw has all 256 tokens in use.
All inputs are finite; a program needn't handle non-finite values.
Results may differ from the reference program's by a relative error of at most 0.006.
The reference program's roundings to bfloat16 on the way (of `packed` and `d_packed`) count: a program that leaves them out, or rounds other values in their place, can miss the bound.
Values may be sent and summed in bfloat16 or wider, within the bound.
A program may use at most 128 MiB of HBM per device.

```python
import math
import jax
import jax.numpy as jnp
from jax import lax

D = 4096
KVH = 4
GQ = 4
HD = 128
LEN = 256
CAND = 4
LISTS = 4


def draw_tokens(key, part):
    key = jax.random.fold_in(key, 5)
    first_key = jax.random.fold_in(key, 0)
    shape = (LISTS, CAND, LEN, D)
    values = jnp.clip(jax.random.normal(first_key, shape, jnp.float32), -6.0, 6.0)
    return values.astype(jnp.bfloat16)


def draw_lengths(key, part):
    key = jax.random.fold_in(key, 11)
    first_key, second_key = jax.random.split(key)
    base_lengths = jax.random.randint(first_key, (LISTS * CAND,), LEN // 4, LEN + 1)
    chosen = jax.random.randint(second_key, (), 0, LISTS * CAND)
    slots = jnp.arange(LISTS * CAND)
    filled = jnp.where(slots == chosen, LEN, base_lengths)
    return filled.reshape(LISTS, CAND).astype(jnp.int32)


def rising_scale(high_log):
    steps = jnp.arange(CAND, dtype=jnp.float32) / max(CAND - 1, 1)
    return jnp.exp(high_log * steps)


def draw_grad_out(key, part):
    key = jax.random.fold_in(key, 17)
    shape = (LISTS, CAND, LEN, KVH, GQ * HD)
    values = jnp.clip(jax.random.normal(key, shape, jnp.float32), -6.0, 6.0)
    factor = rising_scale(math.log(6.0))
    first_pos = (jnp.arange(LEN) == 0).astype(jnp.float32)
    row_scale = 1.0 + (factor[:, None] - 1.0) * first_pos[None, :]
    values = values * row_scale[None, :, :, None, None]
    return values.astype(jnp.bfloat16)


def levels(stream_key, extent, shards, low, largest):
    def one(position, parts):
        heights = jax.random.uniform(jax.random.fold_in(jax.random.fold_in(stream_key, 6), position), (parts,), jnp.float32, low / len(shards), largest / len(shards))
        return jnp.repeat(jnp.exp(heights), extent[position] // parts).reshape((-1,) + (1,) * (len(extent) - position - 1))

    factor_of = one(*shards[0])
    for cut in shards[1:]:
        factor_of = factor_of * one(*cut)
    return factor_of


def gaussian(own_key, dims, deviation, reach, cuts=(), kind=jnp.bfloat16):
    values = jax.random.normal(own_key, dims, jnp.float32) * deviation
    if len(cuts) > 0:
        values = levels(own_key, dims, cuts, -0.22, 0.18) * values
    return jnp.clip(values, min=-reach, max=reach).astype(kind)


def setup_inputs(seed: int = 0) -> dict:
    streams_of = jax.random.split(jax.random.key(seed), 5)
    return {
        "tokens": draw_tokens(jax.random.fold_in(streams_of[4], 71), 0),
        "qkv_weight": gaussian(streams_of[1], (D, KVH, (GQ + 2) * HD), D ** -0.5, 0.09375, ((1, 4),)),
        "lengths": draw_lengths(jax.random.fold_in(streams_of[4], 71), 0),
        "grad_out": draw_grad_out(jax.random.fold_in(streams_of[4], 71), 0),
    }


highest = lax.Precision.HIGHEST
masked_value = -1e+30

def attend(queries, key_rows, value_rows, cls_keys, cls_values, lengths, first_index):
    head_size = queries.shape[-1]
    factor = 1.0 / math.sqrt(head_size)
    cand_total = queries.shape[0]
    seq_len = queries.shape[1]
    listed = cls_keys.shape[0]
    scores = jnp.einsum('clhge,cmhe->chglm', queries, key_rows, precision=highest) * factor
    visible = jnp.arange(seq_len)[None, :] < lengths[:, None]
    scores = jnp.where(visible[:, None, None, None, :], scores, masked_value)
    row_peak = lax.stop_gradient(lax.optimization_barrier(jnp.max(scores, axis=-1, keepdims=True)))
    weights = jnp.exp(scores - row_peak)
    totals = lax.optimization_barrier(jnp.sum(weights, axis=-1))
    blended = jnp.einsum('chglm,cmhe->clhge', weights, value_rows, precision=highest)
    blended = blended / jnp.transpose(totals, (0, 3, 1, 2))[..., None]
    across = jnp.einsum('chge,ahe->chga', queries[:, 0], cls_keys, precision=highest) * factor
    own_slot = jnp.arange(listed)[None, :] == (first_index + jnp.arange(cand_total))[:, None]
    across = jnp.where(own_slot[:, None, None, :], masked_value, across)
    first_row = scores[:, :, :, 0, :]
    joint_peak = lax.stop_gradient(jnp.maximum(lax.optimization_barrier(jnp.max(first_row, axis=-1)), lax.optimization_barrier(jnp.max(across, axis=-1))))[..., None]
    local_weights = jnp.exp(first_row - joint_peak)
    far_weights = jnp.exp(across - joint_peak)
    denominator = lax.optimization_barrier(jnp.sum(local_weights, axis=-1)) + lax.optimization_barrier(jnp.sum(far_weights, axis=-1))
    head_row = jnp.einsum('chgm,cmhe->chge', local_weights, value_rows, precision=highest)
    head_row = head_row + jnp.einsum('chga,ahe->chge', far_weights, cls_values, precision=highest)
    head_row = head_row / denominator[..., None]
    return blended.at[:, 0].set(head_row)

def reference(tokens, qkv_weight, lengths, grad_out):
    list_count, cand_count, seq_len, model_width = tokens.shape
    row_count = list_count * cand_count * seq_len
    flat_rows = tokens.reshape(row_count, model_width)
    weight_mat = qkv_weight.reshape(model_width, -1)
    packed = jnp.dot(flat_rows, weight_mat, preferred_element_type=jnp.float32).astype(jnp.bfloat16)
    packed = packed.reshape(list_count, cand_count, seq_len, KVH, (GQ + 2) * HD)
    queries = packed[..., :GQ * HD].reshape(list_count, cand_count, seq_len, KVH, GQ, HD).astype(jnp.float32)
    key_rows = packed[..., GQ * HD:(GQ + 1) * HD].astype(jnp.float32)
    value_rows = packed[..., (GQ + 1) * HD:].astype(jnp.float32)
    cls_keys = key_rows[:, :, 0]
    cls_values = value_rows[:, :, 0]

    def forward(q_in, k_in, v_in, ck_in, cv_in):
        return jax.vmap(attend, in_axes=(0, 0, 0, 0, 0, 0, None))(q_in, k_in, v_in, ck_in, cv_in, lengths, 0)
    result, pullback = jax.vjp(forward, queries, key_rows, value_rows, cls_keys, cls_values)
    attended = result.reshape(list_count, cand_count, seq_len, KVH, GQ * HD).astype(jnp.bfloat16)
    upstream = grad_out.astype(jnp.float32).reshape(list_count, cand_count, seq_len, KVH, GQ, HD)
    d_query, d_key, d_value, d_cls_key, d_cls_value = pullback(upstream)
    d_key = d_key.at[:, :, 0].add(d_cls_key)
    d_value = d_value.at[:, :, 0].add(d_cls_value)
    d_packed = jnp.concatenate([d_query.reshape(list_count, cand_count, seq_len, KVH, GQ * HD), d_key, d_value], axis=-1)
    d_packed = d_packed.astype(jnp.bfloat16).reshape(row_count, -1)
    grad_x = lax.dot_general(d_packed, weight_mat, (((1,), (1,)), ((), ())), preferred_element_type=jnp.float32)
    grad_x = grad_x.astype(jnp.bfloat16).reshape(tokens.shape)
    grad_w = lax.dot_general(flat_rows, d_packed, (((0,), (0,)), ((), ())), preferred_element_type=jnp.float32)
    return (attended, grad_x, grad_w.reshape(qkv_weight.shape))
```

```python
import functools
import math

import jax
import jax.numpy as jnp
from jax import lax
from jax.experimental import pallas as pl
from jax.experimental.pallas import tpu as pltpu
from jax.sharding import PartitionSpec as P

GQ = 4
HD = 128


highest = lax.Precision.HIGHEST
masked_value = -1e30


def attend(queries, key_rows, value_rows, cls_keys, cls_values, lengths, first_index):
    head_size = queries.shape[-1]
    factor = 1.0 / math.sqrt(head_size)
    cand_total = queries.shape[0]
    seq_len = queries.shape[1]
    listed = cls_keys.shape[0]
    scores = jnp.einsum("clhge,cmhe->chglm", queries, key_rows, precision=highest) * factor
    visible = jnp.arange(seq_len)[None, :] < lengths[:, None]
    scores = jnp.where(visible[:, None, None, None, :], scores, masked_value)
    row_peak = lax.stop_gradient(jnp.max(scores, axis=-1, keepdims=True))
    weights = jnp.exp(scores - row_peak)
    totals = jnp.sum(weights, axis=-1)
    blended = jnp.einsum("chglm,cmhe->clhge", weights, value_rows, precision=highest)
    blended = blended / jnp.transpose(totals, (0, 3, 1, 2))[..., None]
    across = jnp.einsum("chge,ahe->chga", queries[:, 0], cls_keys, precision=highest) * factor
    own_slot = jnp.arange(listed)[None, :] == (first_index + jnp.arange(cand_total))[:, None]
    across = jnp.where(own_slot[:, None, None, :], masked_value, across)
    first_row = scores[:, :, :, 0, :]
    joint_peak = lax.stop_gradient(
        jnp.maximum(jnp.max(first_row, axis=-1), jnp.max(across, axis=-1))
    )[..., None]
    local_weights = jnp.exp(first_row - joint_peak)
    far_weights = jnp.exp(across - joint_peak)
    denominator = jnp.sum(local_weights, axis=-1) + jnp.sum(far_weights, axis=-1)
    head_row = jnp.einsum("chgm,cmhe->chge", local_weights, value_rows, precision=highest)
    head_row = head_row + jnp.einsum("chga,ahe->chge", far_weights, cls_values, precision=highest)
    head_row = head_row / denominator[..., None]
    return blended.at[:, 0].set(head_row)


def body(tokens, qkv_weight, lengths, grad_out):
    list_count, cand_count, seq_len, model_width = tokens.shape
    local_heads = qkv_weight.shape[1]
    row_count = list_count * cand_count * seq_len
    flat_rows = tokens.reshape(row_count, model_width)
    weight_mat = qkv_weight.reshape(model_width, -1)
    packed = jnp.dot(flat_rows, weight_mat, preferred_element_type=jnp.float32).astype(jnp.bfloat16)
    packed = packed.reshape(list_count, cand_count, seq_len, local_heads, (GQ + 2) * HD)
    query_part = packed[..., : GQ * HD].reshape(
        list_count, cand_count, seq_len, local_heads, GQ, HD
    )
    key_part = packed[..., GQ * HD : (GQ + 1) * HD]
    value_part = packed[..., (GQ + 1) * HD :]
    cls_keys, cls_values = (
        lax.all_gather(key_part[:, :, 0], "cand", axis=1, tiled=True),
        lax.all_gather(value_part[:, :, 0], "cand", axis=1, tiled=True),
    )
    first_index = lax.axis_index("cand") * cand_count

    def forward(q_in, k_in, v_in, ck_in, cv_in):
        return jax.vmap(attend, in_axes=(0, 0, 0, 0, 0, 0, None))(
            q_in, k_in, v_in, ck_in, cv_in, lengths, first_index
        )

    result, pullback = jax.vjp(
        forward,
        query_part.astype(jnp.float32),
        key_part.astype(jnp.float32),
        value_part.astype(jnp.float32),
        cls_keys.astype(jnp.float32),
        cls_values.astype(jnp.float32),
    )
    attended = result.reshape(list_count, cand_count, seq_len, local_heads, GQ * HD).astype(
        jnp.bfloat16
    )
    upstream = grad_out.astype(jnp.float32).reshape(
        list_count, cand_count, seq_len, local_heads, GQ, HD
    )
    d_query, d_key, d_value, d_cls_key, d_cls_value = pullback(upstream)
    own_key, own_value = (
        lax.psum_scatter(d_cls_key, "cand", scatter_dimension=1, tiled=True),
        lax.psum_scatter(d_cls_value, "cand", scatter_dimension=1, tiled=True),
    )
    d_key = d_key.at[:, :, 0].add(own_key)
    d_value = d_value.at[:, :, 0].add(own_value)
    d_packed = jnp.concatenate(
        [d_query.reshape(list_count, cand_count, seq_len, local_heads, GQ * HD), d_key, d_value],
        axis=-1,
    )
    d_packed = d_packed.astype(jnp.bfloat16).reshape(row_count, -1)
    partial_x = lax.dot_general(
        d_packed, weight_mat, (((1,), (1,)), ((), ())), preferred_element_type=jnp.float32
    )
    grad_x = lax.psum_scatter(partial_x, "tp", scatter_dimension=1, tiled=True).astype(jnp.bfloat16)
    grad_x = grad_x.reshape(list_count, cand_count, seq_len, -1)
    grad_w = lax.psum_scatter(
        lax.dot_general(
            flat_rows, d_packed, (((0,), (0,)), ((), ())), preferred_element_type=jnp.float32
        ),
        ("cand", "dp"),
        scatter_dimension=0,
        tiled=True,
    )
    return (attended, grad_x, grad_w.reshape(grad_w.shape[0], local_heads, -1))


MESH = pl.DeviceIdType.MESH
f32 = jnp.float32
bf16 = jnp.bfloat16


def dot(a, b, ca, cb):
    return lax.dot_general(a, b, (((ca,), (cb,)), ((), ())), preferred_element_type=f32)


def split(x):
    hi = x.astype(bf16)
    return hi, (x - hi.astype(f32)).astype(bf16)


def dot2(x, b, ca, cb):
    return dot(x[0], b, ca, cb) + dot(x[1], b, ca, cb)


def kernel(
    sizes,
    tok,
    w,
    lens,
    go,
    att,
    gx,
    gw,
    qb,
    kvb,
    cls,
    dcls,
    dclsr,
    dkv_acc,
    gx_acc,
    tokg,
    wg,
    dqz,
    dkvz,
    dqp,
    dkvp,
    cls_s,
    cls_r,
    dcls_s,
    dcls_r,
    tok_s,
    tok_r,
    wz_s,
    wz_r,
    wp_s,
    wp_r,
    wf_s,
    z_s,
    z_r,
    zf_s,
    p_s,
    p_r,
    pf_s,
):
    nc, nt, nd, own, length = sizes
    ne = nc * nd
    c, t, d = lax.axis_index("cand"), lax.axis_index("tp"), lax.axis_index("dp")
    e = c * nd + d
    sib = d + 1 - 2 * lax.rem(d, 2)
    cols = tok.shape[1] // ne
    xcols = w.shape[0] // nt
    part = xcols // ne
    rows = own * length
    scale = 1.0 / math.sqrt(HD)

    cls[...] = jnp.zeros_like(cls)
    dcls[...] = jnp.zeros_like(dcls)
    dkv_acc[...] = jnp.zeros_like(dkv_acc)

    def plane(k):
        j = lax.rem(e + k, ne)
        return j, {"cand": j // nd, "dp": lax.rem(j, nd)}

    nh = nd // 2

    def chip(k):
        j = lax.rem(c * nh + d // 2 + k, nc * nh)
        jc, jd = j // nh, 2 * lax.rem(j, nh) + lax.rem(d, 2)
        return jc * nd + jd, {"cand": jc, "dp": jd}

    barrier = pltpu.get_barrier_semaphore()
    for k in range(1, ne):
        pl.semaphore_signal(barrier, inc=1, device_id=plane(k)[1], device_id_type=MESH)
    for k in range(1, nt):
        pl.semaphore_signal(
            barrier, inc=1, device_id={"tp": lax.rem(t + k, nt)}, device_id_type=MESH
        )
    pl.semaphore_wait(barrier, ne - 1 + nt - 1)

    def remote(src, dst, ss, rs, dev):
        return pltpu.make_async_remote_copy(
            src_ref=src, dst_ref=dst, send_sem=ss, recv_sem=rs, device_id=dev, device_id_type=MESH
        )

    def wz_send(k):
        o = lax.rem(t + k, nt)
        return remote(
            w.at[pl.ds(pl.multiple_of(o * xcols + e * part, 16), part)],
            wg.at[t, e],
            wz_s.at[k],
            wz_r.at[t],
            {"tp": o},
        )

    def wz_recv(k):
        h = lax.rem(t + k, nt)
        return remote(wg.at[h, e], wg.at[h, e], wz_s.at[k], wz_r.at[h], {"tp": h})

    def wp_send(k, h):
        return remote(wg.at[h, e], wg.at[h, e], wp_s.at[k, h], wp_r.at[e, h], chip(k)[1])

    def wp_sib(j, k, h):
        return remote(wg.at[h, j], wg.at[h, j], wf_s.at[k, h], wp_r.at[j, h], {"dp": sib})

    def w_wait(j, h):
        remote(wg.at[h, j], wg.at[h, j], wf_s.at[0, h], wp_r.at[j, h], {"dp": sib}).wait_recv()

    def tok_send(k):
        j, dev = plane(k)
        return remote(
            tok.at[:, pl.ds(pl.multiple_of(j * cols, 128), cols)],
            tokg.at[e],
            tok_s.at[k],
            tok_r.at[e],
            dev,
        )

    for k in range(1, nt):
        wz_send(k).start()
    for k in range(1, ne):
        tok_send(k).start()

    def zbuf(n, s):
        return dqz.at[s, n] if n < own else dkvz.at[s]

    def pbuf(n, s):
        return dqp.at[s, n] if n < own else dkvp.at[s]

    def z_copy(n, s, to, ss):
        return remote(zbuf(n, s), zbuf(n, s), ss, z_r.at[n, s], {"tp": to})

    def p_send(n, k):
        return remote(zbuf(n, t), pbuf(n, e), p_s.at[n, k], p_r.at[n, e], chip(k)[1])

    def p_sib(n):
        return remote(zbuf(n, t), pbuf(n, e), pf_s.at[n, 0], p_r.at[n, e], {"dp": sib})

    def p_fwd(n, j, k):
        return remote(pbuf(n, j), pbuf(n, j), pf_s.at[n, k], p_r.at[n, j], {"dp": sib})

    def p_wait(n, j):
        remote(pbuf(n, j), pbuf(n, j), pf_s.at[n, 0], p_r.at[n, j], {"dp": sib}).wait_recv()

    def send_chunk(n):
        for side in (0, 1):
            to = t + 2 * side - 1

            @pl.when((to >= 0) & (to < nt))
            def _():
                z_copy(n, t, to, z_s.at[n, side]).start()

        for k in range(1, nc * nh):
            p_send(n, k).start()
        p_sib(n).start()

    kvb[...] = dot(tok[...], w[:, GQ * HD :], 1, 0).astype(bf16)
    first = lax.broadcasted_iota(jnp.int32, (16, 2 * HD), 0)
    mine = jnp.zeros((16, 2 * HD), f32)
    for p in range(own):
        row = kvb[p * length : p * length + 16, :].astype(f32)[0:1]
        mine = jnp.where(first == p, row, mine)
    c16 = pl.ds(pl.multiple_of(c * 16, 16), 16)
    cls[c16, :] = mine.astype(bf16)

    def cls_send(k):
        return remote(
            cls.at[c16], cls.at[c16], cls_s.at[k], cls_r.at[c], {"cand": lax.rem(c + k, nc)}
        )

    def cls_recv(k):
        o = lax.rem(c + k, nc)
        o16 = pl.ds(pl.multiple_of(o * 16, 16), 16)
        return remote(cls.at[o16], cls.at[o16], cls_s.at[k], cls_r.at[o], {"cand": o})

    for k in range(1, nc):
        cls_send(k).start()

    @pl.loop(0, GQ * HD // 256)
    def _(i):
        at = pl.ds(pl.multiple_of(i * 256, 256), 256)
        qb[:, at] = dot(tok[...], w[:, at], 1, 0).astype(bf16)

    for k in range(1, nc):
        cls_recv(k).wait_recv()

    far_lane = lax.broadcasted_iota(jnp.int32, (16, 128), 1)
    far_row = lax.broadcasted_iota(jnp.int32, (16, 128), 0)
    lane = lax.broadcasted_iota(jnp.int32, (length, length), 1)

    for p in range(own):
        at = slice(p * length, (p + 1) * length)
        visible = lane < lens[p]
        listed = (far_row == 0) & (lax.rem(far_lane, 16) < own) & (far_lane < nc * 16)
        listed = listed & (far_lane != c * 16 + p)

        @pl.loop(0, GQ)
        def _(g):
            head = pl.ds(pl.multiple_of(g * HD, HD), HD)
            q, do = qb[at, head], go[at, head]
            k, v = kvb[at, :HD], kvb[at, HD:]
            ck, cv = cls[:, :HD], cls[:, HD:]
            q16, do16 = q[:16], do[:16]
            s = jnp.where(visible, dot(q, k, 1, 1) * scale, masked_value)
            f = jnp.where(listed, dot(q16, ck, 1, 1) * scale, masked_value)
            m = jnp.max(s, axis=1, keepdims=True)
            m16 = jnp.maximum(m[:16], jnp.max(f, axis=1, keepdims=True))
            m = jnp.concatenate([m16, m[16:]], axis=0)
            pr, pf = jnp.exp(s - m), jnp.exp(f - m16)
            total = jnp.sum(pr, axis=1, keepdims=True)
            t16 = total[:16] + jnp.sum(pf, axis=1, keepdims=True)
            total = jnp.concatenate([t16, total[16:]], axis=0)
            pr, pf = pr / total, pf / t16
            prs, pfs = split(pr), split(pf)
            o = dot2(prs, v, 1, 0)
            o = jnp.concatenate([o[:16] + dot2(pfs, cv, 1, 0), o[16:]], axis=0)
            att[at, head] = o.astype(bf16)
            delta = jnp.sum(o * do.astype(f32), axis=1, keepdims=True)
            ds = split(pr * (dot(do, v, 1, 1) - delta) * scale)
            dsf = split(pf * (dot(do16, cv, 1, 1) - delta[:16]) * scale)
            dq = dot2(ds, k, 1, 0)
            dq = jnp.concatenate([dq[:16] + dot2(dsf, ck, 1, 0), dq[16:]], axis=0)
            dqz[t, p, :, head] = dq.astype(bf16)
            dkv_acc[at, :HD] += dot2(ds, q, 0, 0)
            dkv_acc[at, HD:] += dot2(prs, do, 0, 0)
            dcls[:, :HD] += dot2(dsf, q16, 0, 0)
            dcls[:, HD:] += dot2(pfs, do16, 0, 0)

        if p == own - 1:
            def dcls_send(k):
                o = lax.rem(c + k, nc)
                o16 = pl.ds(pl.multiple_of(o * 16, 16), 16)
                return remote(dcls.at[o16], dclsr.at[c], dcls_s.at[k], dcls_r.at[c], {"cand": o})

            for k in range(1, nc):
                dcls_send(k).start()
        send_chunk(p)
        if p == 0:
            for k in range(1, nt):
                wz_recv(k).wait_recv()
            for k in range(1, nt):
                h = lax.rem(t + k, nt)
                for j in range(1, nc * nh):
                    wp_send(j, h).start()
                wp_sib(e, 0, h).start()

    mine = dcls[c16, :]
    for k in range(1, nc):
        o = lax.rem(c + k, nc)
        remote(dclsr.at[o], dclsr.at[o], dcls_s.at[k], dcls_r.at[o], {"cand": o}).wait_recv()
        mine = mine + dclsr[o]
    top = lax.broadcasted_iota(jnp.int32, (8, 2 * HD), 0)
    for p in range(own):
        at = slice(p * length, p * length + 8)
        dkv_acc[at, :] = dkv_acc[at, :] + jnp.where(top == 0, mine[p : p + 1], 0.0)
    dkvz[t] = dkv_acc[...].astype(bf16)
    send_chunk(own)

    def x_terms(h, weight, start):
        @pl.loop(0, xcols // part)
        def _(i):
            wi = weight(i)
            at = pl.ds(pl.multiple_of(i * part, 128), part)
            for p in range(own):
                rs = slice(p * length, (p + 1) * length)
                y = dot(dqz[h, p], wi[:, : GQ * HD], 1, 1)
                y = y + dot(dkvz[h, rs, :], wi[:, GQ * HD :], 1, 1)
                if start:
                    gx_acc[rs, at] = y
                else:
                    gx_acc[rs, at] += y

    def w_terms(x, dq, dkv, start):
        xs = [x[p * length : (p + 1) * length] for p in range(own)]
        y = dot(xs[0], dq(0), 0, 0)
        for p in range(1, own):
            y = y + dot(xs[p], dq(p), 0, 0)
        z = dot(x, dkv, 0, 0)
        if start:
            gw[:, : GQ * HD] = y
            gw[:, GQ * HD :] = z
        else:
            gw[:, : GQ * HD] += y
            gw[:, GQ * HD :] += z

    x_terms(
        t, lambda i: w[pl.ds(pl.multiple_of(t * xcols + i * part, 16), part), :], True
    )
    w_terms(
        tok[:, pl.ds(pl.multiple_of(e * cols, 128), cols)],
        lambda p: dqz[t, p],
        dkvz[t],
        True,
    )

    for n in range(own + 1):
        for k in range(1, nc * nh):
            j = chip(k)[0]
            p_wait(n, j)
            p_fwd(n, j, k).start()
        for side in (0, 1):
            src, to = t + 2 * side - 1, t - 2 * side + 1

            @pl.when((src >= 0) & (src < nt))
            def _():
                z_copy(n, src, t, zf_s.at[n, 1, side]).wait_recv()

                @pl.when((to >= 0) & (to < nt))
                def _():
                    z_copy(n, src, to, zf_s.at[n, 1, side]).start()

    for k in range(1, nc * nh):
        j = chip(k)[0]
        for i in range(1, nt):
            h = lax.rem(t + i, nt)
            w_wait(j, h)
            wp_sib(j, k, h).start()

    for dist in range(2, nt):
        for n in range(own + 1):
            for side in (0, 1):
                src, to = t + dist * (2 * side - 1), t - 2 * side + 1

                @pl.when((src >= 0) & (src < nt))
                def _():
                    z_copy(n, src, t, zf_s.at[n, dist, side]).wait_recv()
                    if dist < nt - 1:

                        @pl.when((to >= 0) & (to < nt))
                        def _():
                            z_copy(n, src, to, zf_s.at[n, dist, side]).start()

    for k in range(nc * nh):
        j = chip(k)[0]
        js = j + 1 - 2 * lax.rem(d, 2)
        for i in range(1, nt):
            w_wait(js, lax.rem(t + i, nt))

    @pl.loop(1, nt)
    def _(i):
        h = lax.rem(t + i, nt)
        x_terms(h, lambda i: wg[h, i], False)

    gx[...] = gx_acc[...].astype(bf16)

    for k in range(nc * nh):
        j = chip(k)[0]
        js = j + 1 - 2 * lax.rem(d, 2)
        for n in range(own + 1):
            p_wait(n, js)
    for k in range(1, ne):
        j = plane(k)[0]
        remote(tokg.at[j], tokg.at[j], tok_s.at[k], tok_r.at[j], {"dp": sib}).wait_recv()

    @pl.loop(1, ne)
    def _(k):
        j = lax.rem(e + k, ne)
        w_terms(tokg[j], lambda p: dqp[j, p], dkvp[j], False)

    for k in range(1, nt):
        wz_send(k).wait_send()
    for k in range(1, ne):
        tok_send(k).wait_send()
    for k in range(1, nc):
        cls_send(k).wait_send()
        o = lax.rem(c + k, nc)
        o16 = pl.ds(pl.multiple_of(o * 16, 16), 16)
        remote(dcls.at[o16], dclsr.at[c], dcls_s.at[k], dcls_r.at[c], {"cand": o}).wait_send()
    for i in range(1, nt):
        h = lax.rem(t + i, nt)
        for k in range(1, nc * nh):
            wp_send(k, h).wait_send()
            wp_sib(chip(k)[0], k, h).wait_send()
        wp_sib(e, 0, h).wait_send()
    for n in range(own + 1):
        for side in (0, 1):
            to = t + 2 * side - 1

            @pl.when((to >= 0) & (to < nt))
            def _():
                z_copy(n, t, to, z_s.at[n, side]).wait_send()

            for dist in range(1, nt - 1):
                src, on = t + dist * (2 * side - 1), t - 2 * side + 1

                @pl.when((src >= 0) & (src < nt) & (on >= 0) & (on < nt))
                def _():
                    z_copy(n, src, on, zf_s.at[n, dist, side]).wait_send()

        for k in range(1, nc * nh):
            p_send(n, k).wait_send()
            p_fwd(n, chip(k)[0], k).wait_send()
        p_sib(n).wait_send()


def fused(sizes, tokens, qkv_weight, lengths, grad_out):
    nc, nt, nd, own, length = sizes
    ne, width, rows = nc * nd, tokens.shape[-1], own * length
    cols, xcols = width // ne, width // nt
    kv, heads = 2 * HD, GQ * HD
    dma = pltpu.SemaphoreType.DMA
    vmem = pl.BlockSpec(memory_space=pltpu.VMEM)
    flops = 6 * rows * width * (heads + kv)
    attended, grad_x, grad_w = pl.pallas_call(
        functools.partial(kernel, sizes),
        out_shape=(
            jax.ShapeDtypeStruct((rows, heads), bf16),
            jax.ShapeDtypeStruct((rows, xcols), bf16),
            jax.ShapeDtypeStruct((cols, heads + kv), f32),
        ),
        in_specs=[vmem, vmem, pl.BlockSpec(memory_space=pltpu.SMEM), vmem],
        out_specs=(vmem, vmem, vmem),
        scratch_shapes=[
            pltpu.VMEM((rows, heads), bf16),
            pltpu.VMEM((rows, kv), bf16),
            pltpu.VMEM((128, kv), bf16),
            pltpu.VMEM((128, kv), f32),
            pltpu.VMEM((nc, 16, kv), f32),
            pltpu.VMEM((rows, kv), f32),
            pltpu.VMEM((rows, xcols), f32),
            pltpu.VMEM((ne, rows, cols), bf16),
            pltpu.VMEM((nt, ne, xcols // ne, heads + kv), bf16),
            pltpu.VMEM((nt, own, length, heads), bf16),
            pltpu.VMEM((nt, rows, kv), bf16),
            pltpu.VMEM((ne, own, length, heads), bf16),
            pltpu.VMEM((ne, rows, kv), bf16),
            dma((nc,)),
            dma((nc,)),
            dma((nc,)),
            dma((nc,)),
            dma((ne,)),
            dma((ne,)),
            dma((nt,)),
            dma((nt,)),
            dma((ne // 2, nt)),
            dma((ne, nt)),
            dma((ne // 2, nt)),
            dma((own + 1, 2)),
            dma((own + 1, nt)),
            dma((own + 1, nt, 2)),
            dma((own + 1, ne // 2)),
            dma((own + 1, ne)),
            dma((own + 1, ne // 2)),
        ],
        compiler_params=pltpu.CompilerParams(
            collective_id=0, has_side_effects=True, vmem_limit_bytes=58 * 2**20
        ),
        cost_estimate=pl.CostEstimate(
            flops=flops, bytes_accessed=16 * 2**20, transcendentals=rows * length * GQ
        ),
    )(
        tokens.reshape(rows, width),
        qkv_weight.reshape(width, heads + kv),
        lengths.reshape(own),
        grad_out.reshape(rows, heads),
    )
    return (
        attended.reshape(1, own, length, 1, heads),
        grad_x.reshape(1, own, length, xcols),
        grad_w.reshape(cols, 1, heads + kv),
    )


def local(sizes, tokens, qkv_weight, lengths, grad_out):
    nc, nt, nd = sizes
    lists, own, length, width = tokens.shape
    ne = nc * nd
    fits = (
        lists == 1
        and qkv_weight.shape[1] == 1
        and nd % 2 == 0
        and nc * 16 <= 128
        and own <= 8
        and width % (ne * 128) == 0
        and width % (ne * nt * 128) == 0
        and length % 128 == 0
        and 2 * ne * own * length * (width // ne) <= 6 * 2**20
    )
    if fits:
        return fused((nc, nt, nd, own, length), tokens, qkv_weight, lengths, grad_out)
    return body(tokens, qkv_weight, lengths, grad_out)


def solution(mesh):
    placed = (
        P("dp", "cand", None, None),
        P(None, "tp", None),
        P("dp", "cand"),
        P("dp", "cand", None, "tp", None),
    )
    sizes = tuple(mesh.shape[name] for name in ("cand", "tp", "dp"))
    return jax.shard_map(
        functools.partial(local, sizes),
        mesh=mesh,
        in_specs=placed,
        out_specs=(
            P("dp", "cand", None, "tp", None),
            P("dp", "cand", None, "tp"),
            P(("cand", "dp"), "tp", None),
        ),
        check_vma=False,
    )
```

```python
import functools
import math

import jax
import jax.numpy as jnp
from jax import lax
from jax.experimental import pallas as pl
from jax.experimental.pallas import tpu as pltpu
from jax.sharding import PartitionSpec as P

GQ = 4
HD = 128


highest = lax.Precision.HIGHEST
masked_value = -1e30


def attend(queries, key_rows, value_rows, cls_keys, cls_values, lengths, first_index):
    head_size = queries.shape[-1]
    factor = 1.0 / math.sqrt(head_size)
    cand_total = queries.shape[0]
    seq_len = queries.shape[1]
    listed = cls_keys.shape[0]
    scores = jnp.einsum("clhge,cmhe->chglm", queries, key_rows, precision=highest) * factor
    visible = jnp.arange(seq_len)[None, :] < lengths[:, None]
    scores = jnp.where(visible[:, None, None, None, :], scores, masked_value)
    row_peak = lax.stop_gradient(jnp.max(scores, axis=-1, keepdims=True))
    weights = jnp.exp(scores - row_peak)
    totals = jnp.sum(weights, axis=-1)
    blended = jnp.einsum("chglm,cmhe->clhge", weights, value_rows, precision=highest)
    blended = blended / jnp.transpose(totals, (0, 3, 1, 2))[..., None]
    across = jnp.einsum("chge,ahe->chga", queries[:, 0], cls_keys, precision=highest) * factor
    own_slot = jnp.arange(listed)[None, :] == (first_index + jnp.arange(cand_total))[:, None]
    across = jnp.where(own_slot[:, None, None, :], masked_value, across)
    first_row = scores[:, :, :, 0, :]
    joint_peak = lax.stop_gradient(
        jnp.maximum(jnp.max(first_row, axis=-1), jnp.max(across, axis=-1))
    )[..., None]
    local_weights = jnp.exp(first_row - joint_peak)
    far_weights = jnp.exp(across - joint_peak)
    denominator = jnp.sum(local_weights, axis=-1) + jnp.sum(far_weights, axis=-1)
    head_row = jnp.einsum("chgm,cmhe->chge", local_weights, value_rows, precision=highest)
    head_row = head_row + jnp.einsum("chga,ahe->chge", far_weights, cls_values, precision=highest)
    head_row = head_row / denominator[..., None]
    return blended.at[:, 0].set(head_row)


def body(tokens, qkv_weight, lengths, grad_out):
    list_count, cand_count, seq_len, model_width = tokens.shape
    local_heads = qkv_weight.shape[1]
    row_count = list_count * cand_count * seq_len
    flat_rows = tokens.reshape(row_count, model_width)
    weight_mat = qkv_weight.reshape(model_width, -1)
    packed = jnp.dot(flat_rows, weight_mat, preferred_element_type=jnp.float32).astype(jnp.bfloat16)
    packed = packed.reshape(list_count, cand_count, seq_len, local_heads, (GQ + 2) * HD)
    query_part = packed[..., : GQ * HD].reshape(
        list_count, cand_count, seq_len, local_heads, GQ, HD
    )
    key_part = packed[..., GQ * HD : (GQ + 1) * HD]
    value_part = packed[..., (GQ + 1) * HD :]
    cls_keys, cls_values = (
        lax.all_gather(key_part[:, :, 0], "cand", axis=1, tiled=True),
        lax.all_gather(value_part[:, :, 0], "cand", axis=1, tiled=True),
    )
    first_index = lax.axis_index("cand") * cand_count

    def forward(q_in, k_in, v_in, ck_in, cv_in):
        return jax.vmap(attend, in_axes=(0, 0, 0, 0, 0, 0, None))(
            q_in, k_in, v_in, ck_in, cv_in, lengths, first_index
        )

    result, pullback = jax.vjp(
        forward,
        query_part.astype(jnp.float32),
        key_part.astype(jnp.float32),
        value_part.astype(jnp.float32),
        cls_keys.astype(jnp.float32),
        cls_values.astype(jnp.float32),
    )
    attended = result.reshape(list_count, cand_count, seq_len, local_heads, GQ * HD).astype(
        jnp.bfloat16
    )
    upstream = grad_out.astype(jnp.float32).reshape(
        list_count, cand_count, seq_len, local_heads, GQ, HD
    )
    d_query, d_key, d_value, d_cls_key, d_cls_value = pullback(upstream)
    own_key, own_value = (
        lax.psum_scatter(d_cls_key, "cand", scatter_dimension=1, tiled=True),
        lax.psum_scatter(d_cls_value, "cand", scatter_dimension=1, tiled=True),
    )
    d_key = d_key.at[:, :, 0].add(own_key)
    d_value = d_value.at[:, :, 0].add(own_value)
    d_packed = jnp.concatenate(
        [d_query.reshape(list_count, cand_count, seq_len, local_heads, GQ * HD), d_key, d_value],
        axis=-1,
    )
    d_packed = d_packed.astype(jnp.bfloat16).reshape(row_count, -1)
    partial_x = lax.dot_general(
        d_packed, weight_mat, (((1,), (1,)), ((), ())), preferred_element_type=jnp.float32
    )
    grad_x = lax.psum_scatter(partial_x, "tp", scatter_dimension=1, tiled=True).astype(jnp.bfloat16)
    grad_x = grad_x.reshape(list_count, cand_count, seq_len, -1)
    grad_w = lax.psum_scatter(
        lax.dot_general(
            flat_rows, d_packed, (((0,), (0,)), ((), ())), preferred_element_type=jnp.float32
        ),
        ("cand", "dp"),
        scatter_dimension=0,
        tiled=True,
    )
    return (attended, grad_x, grad_w.reshape(grad_w.shape[0], local_heads, -1))


MESH = pl.DeviceIdType.MESH
f32 = jnp.float32
bf16 = jnp.bfloat16


def dot(a, b, ca, cb):
    return lax.dot_general(a, b, (((ca,), (cb,)), ((), ())), preferred_element_type=f32)


def split(x):
    hi = x.astype(bf16)
    return hi, (x - hi.astype(f32)).astype(bf16)


def dot2(x, b, ca, cb):
    return dot(x[0], b, ca, cb) + dot(x[1], b, ca, cb)


def kernel(
    sizes,
    tok,
    w,
    lens,
    go,
    att,
    gx,
    gw,
    qb,
    kvb,
    cls,
    dcls,
    dclsr,
    dkv_acc,
    gx_acc,
    tokg,
    wg,
    dqz,
    dkvz,
    dqp,
    dkvp,
    gsq,
    gsk,
    grq,
    grk,
    cls_s,
    cls_r,
    dcls_s,
    dcls_r,
    tok_s,
    tok_r,
    wz_s,
    wz_r,
    wp_s,
    wp_r,
    wf_s,
    z_s,
    z_r,
    zf_s,
    p_s,
    p_r,
    pf_s,
    g_s,
    g_r,
):
    nc, nt, nd, own, length = sizes
    ny, nx = nd // 2, nc * 2
    c, t, d = lax.axis_index("cand"), lax.axis_index("tp"), lax.axis_index("dp")
    y, core = d // 2, lax.rem(d, 2)
    sib = d + 1 - 2 * core
    me = c * 2 + core
    cols = tok.shape[1] // (nc * nd)
    xcols = w.shape[0] // nt
    part = xcols // nd
    heads = GQ * HD
    scale = 1.0 / math.sqrt(HD)

    cls[...] = jnp.zeros_like(cls)
    dcls[...] = jnp.zeros_like(dcls)
    dkv_acc[...] = jnp.zeros_like(dkv_acc)

    def row(k):
        j = lax.rem(me + k, nx)
        return j, {"cand": j // 2, "dp": 2 * y + lax.rem(j, 2)}

    def along(k):
        j = lax.rem(c + k, nc)
        return j * 2 + core, {"cand": j}

    def across(k):
        j = 2 * lax.rem(y + k, ny) + core
        return j, {"dp": j}

    barrier = pltpu.get_barrier_semaphore()
    for k in range(1, nx):
        pl.semaphore_signal(barrier, inc=1, device_id=row(k)[1], device_id_type=MESH)
    for k in range(1, ny):
        pl.semaphore_signal(barrier, inc=1, device_id=across(k)[1], device_id_type=MESH)
    for k in range(1, nt):
        pl.semaphore_signal(
            barrier, inc=1, device_id={"tp": lax.rem(t + k, nt)}, device_id_type=MESH
        )
    pl.semaphore_wait(barrier, nx - 1 + ny - 1 + nt - 1)

    def remote(src, dst, ss, rs, dev):
        return pltpu.make_async_remote_copy(
            src_ref=src, dst_ref=dst, send_sem=ss, recv_sem=rs, device_id=dev, device_id_type=MESH
        )

    def wz_send(k):
        o = lax.rem(t + k, nt)
        return remote(
            w.at[pl.ds(pl.multiple_of(o * xcols + d * part, 16), part)],
            wg.at[t, d],
            wz_s.at[k],
            wz_r.at[t],
            {"tp": o},
        )

    def wz_recv(k):
        h = lax.rem(t + k, nt)
        return remote(wg.at[h, d], wg.at[h, d], wz_s.at[k], wz_r.at[h], {"tp": h})

    def wp_send(k, h):
        return remote(wg.at[h, d], wg.at[h, d], wp_s.at[k, h], wp_r.at[d, h], across(k)[1])

    def wp_sib(j, k, h):
        return remote(wg.at[h, j], wg.at[h, j], wf_s.at[k, h], wp_r.at[j, h], {"dp": sib})

    def w_wait(j, h):
        remote(wg.at[h, j], wg.at[h, j], wf_s.at[0, h], wp_r.at[j, h], {"dp": sib}).wait_recv()

    def block(cc, step, kk):
        j = cc * nd + 2 * lax.rem(y + step, ny) + kk
        return pl.ds(pl.multiple_of(j * cols, 128), cols)

    def tok_send(step, k):
        j, dev = row(k)
        return remote(
            tok.at[:, block(j // 2, step, lax.rem(j, 2))],
            tokg.at[step, me],
            tok_s.at[step, k],
            tok_r.at[step, me],
            dev,
        )

    def tok_wait(step):
        for k in range(1, nx):
            j, dev = row(k)
            remote(
                tokg.at[step, j], tokg.at[step, j], tok_s.at[step, k], tok_r.at[step, j], dev
            ).wait_recv()

    for k in range(1, nt):
        wz_send(k).start()
    for step in range(1, ny):
        for k in range(1, nx):
            tok_send(step, k).start()

    def zbuf(n, s):
        return dqz.at[s, n] if n < own else dkvz.at[s]

    def pbuf(n, s):
        return dqp.at[s, n] if n < own else dkvp.at[s]

    def z_copy(n, s, to, ss):
        return remote(zbuf(n, s), zbuf(n, s), ss, z_r.at[n, s], {"tp": to})

    def p_send(n, k):
        return remote(zbuf(n, t), pbuf(n, me), p_s.at[n, k], p_r.at[n, me], along(k)[1])

    def p_sib(n):
        return remote(zbuf(n, t), pbuf(n, me), pf_s.at[n, 0], p_r.at[n, me], {"dp": sib})

    def p_fwd(n, j, k):
        return remote(pbuf(n, j), pbuf(n, j), pf_s.at[n, k], p_r.at[n, j], {"dp": sib})

    def p_wait(n, j):
        remote(pbuf(n, j), pbuf(n, j), pf_s.at[n, 0], p_r.at[n, j], {"dp": sib}).wait_recv()

    def send_chunk(n):
        for side in (0, 1):
            to = t + 2 * side - 1

            @pl.when((to >= 0) & (to < nt))
            def _():
                z_copy(n, t, to, z_s.at[n, side]).start()

        for k in range(1, nc):
            p_send(n, k).start()
        p_sib(n).start()

    kvb[...] = dot(tok[...], w[:, heads:], 1, 0).astype(bf16)
    first = lax.broadcasted_iota(jnp.int32, (16, 2 * HD), 0)
    mine = jnp.zeros((16, 2 * HD), f32)
    for p in range(own):
        cls_row = kvb[p * length : p * length + 16, :].astype(f32)[0:1]
        mine = jnp.where(first == p, cls_row, mine)

    def rows_of(j):
        return pl.ds(pl.multiple_of(j * 16, 16), 16)

    cls[rows_of(c), :] = mine.astype(bf16)

    def cls_send(k):
        return remote(
            cls.at[rows_of(c)], cls.at[rows_of(c)], cls_s.at[k], cls_r.at[c], along(k)[1]
        )

    def cls_recv(k):
        o = lax.rem(c + k, nc)
        return remote(cls.at[rows_of(o)], cls.at[rows_of(o)], cls_s.at[k], cls_r.at[o], {"cand": o})

    def dcls_send(k):
        o = lax.rem(c + k, nc)
        return remote(dcls.at[rows_of(o)], dclsr.at[c], dcls_s.at[k], dcls_r.at[c], {"cand": o})

    for k in range(1, nc):
        cls_send(k).start()

    @pl.loop(0, heads // 256)
    def _(i):
        at = pl.ds(pl.multiple_of(i * 256, 256), 256)
        qb[:, at] = dot(tok[...], w[:, at], 1, 0).astype(bf16)

    for k in range(1, nc):
        cls_recv(k).wait_recv()

    far_lane = lax.broadcasted_iota(jnp.int32, (16, 128), 1)
    far_row = lax.broadcasted_iota(jnp.int32, (16, 128), 0)
    lane = lax.broadcasted_iota(jnp.int32, (length, length), 1)

    for p in range(own):
        at = slice(p * length, (p + 1) * length)
        visible = lane < lens[p]
        listed = (far_row == 0) & (lax.rem(far_lane, 16) < own) & (far_lane < nc * 16)
        listed = listed & (far_lane != c * 16 + p)

        @pl.loop(0, GQ)
        def _(g):
            head = pl.ds(pl.multiple_of(g * HD, HD), HD)
            q, do = qb[at, head], go[at, head]
            k, v = kvb[at, :HD], kvb[at, HD:]
            ck, cv = cls[:, :HD], cls[:, HD:]
            q16, do16 = q[:16], do[:16]
            s = jnp.where(visible, dot(q, k, 1, 1) * scale, masked_value)
            f = jnp.where(listed, dot(q16, ck, 1, 1) * scale, masked_value)
            m = jnp.max(s, axis=1, keepdims=True)
            m16 = jnp.maximum(m[:16], jnp.max(f, axis=1, keepdims=True))
            m = jnp.concatenate([m16, m[16:]], axis=0)
            pr, pf = jnp.exp(s - m), jnp.exp(f - m16)
            total = jnp.sum(pr, axis=1, keepdims=True)
            t16 = total[:16] + jnp.sum(pf, axis=1, keepdims=True)
            total = jnp.concatenate([t16, total[16:]], axis=0)
            pr, pf = pr / total, pf / t16
            prs, pfs = split(pr), split(pf)
            o = dot2(prs, v, 1, 0)
            o = jnp.concatenate([o[:16] + dot2(pfs, cv, 1, 0), o[16:]], axis=0)
            att[at, head] = o.astype(bf16)
            delta = jnp.sum(o * do.astype(f32), axis=1, keepdims=True)
            ds = split(pr * (dot(do, v, 1, 1) - delta) * scale)
            dsf = split(pf * (dot(do16, cv, 1, 1) - delta[:16]) * scale)
            dq = dot2(ds, k, 1, 0)
            dq = jnp.concatenate([dq[:16] + dot2(dsf, ck, 1, 0), dq[16:]], axis=0)
            dqz[t, p, :, head] = dq.astype(bf16)
            dkv_acc[at, :HD] += dot2(ds, q, 0, 0)
            dkv_acc[at, HD:] += dot2(prs, do, 0, 0)
            dcls[:, :HD] += dot2(dsf, q16, 0, 0)
            dcls[:, HD:] += dot2(pfs, do16, 0, 0)

        if p == own - 1:
            for k in range(1, nc):
                dcls_send(k).start()
        send_chunk(p)

    mine = dcls[rows_of(c), :]
    for k in range(1, nc):
        o = lax.rem(c + k, nc)
        remote(dclsr.at[o], dclsr.at[o], dcls_s.at[k], dcls_r.at[o], {"cand": o}).wait_recv()
        mine = mine + dclsr[o]
    top = lax.broadcasted_iota(jnp.int32, (8, 2 * HD), 0)
    for p in range(own):
        at = slice(p * length, p * length + 8)
        dkv_acc[at, :] = dkv_acc[at, :] + jnp.where(top == 0, mine[p : p + 1], 0.0)
    dkvz[t] = dkv_acc[...].astype(bf16)
    send_chunk(own)
    for k in range(1, nx):
        tok_send(0, k).start()

    def x_terms(h, weight, start):
        @pl.loop(0, nd)
        def _(i):
            wi = weight(i)
            at = pl.ds(pl.multiple_of(i * part, 128), part)
            for p in range(own):
                rs = slice(p * length, (p + 1) * length)
                v = dot(dqz[h, p], wi[:, :heads], 1, 1)
                v = v + dot(dkvz[h, rs, :], wi[:, heads:], 1, 1)
                if start:
                    gx_acc[rs, at] = v
                else:
                    gx_acc[rs, at] += v

    def q_terms(x, dq):
        v = dot(x[:length], dq(0), 0, 0)
        for p in range(1, own):
            v = v + dot(x[p * length : (p + 1) * length], dq(p), 0, 0)
        return v

    def own_cols(step):
        return tok[:, block(c, step, core)]

    x_terms(t, lambda i: w[pl.ds(pl.multiple_of(t * xcols + i * part, 16), part), :], True)
    for step in range(1, ny):
        x = own_cols(step)
        gsq[step - 1] = q_terms(x, lambda p: dqz[t, p])
        gsk[step - 1] = dot(x, dkvz[t], 0, 0)
    x = own_cols(0)
    gw[:, :heads] = q_terms(x, lambda p: dqz[t, p])
    gw[:, heads:] = dot(x, dkvz[t], 0, 0)

    def z_pass(n, dist):
        for side in (0, 1):
            src, to = t + dist * (2 * side - 1), t - 2 * side + 1

            @pl.when((src >= 0) & (src < nt))
            def _():
                z_copy(n, src, t, zf_s.at[n, dist, side]).wait_recv()
                if dist < nt - 1:

                    @pl.when((to >= 0) & (to < nt))
                    def _():
                        z_copy(n, src, to, zf_s.at[n, dist, side]).start()

    for n in range(own + 1):
        z_pass(n, 1)
        for k in range(1, nc):
            j = along(k)[0]
            p_wait(n, j)
            p_fwd(n, j, k).start()
    for k in range(1, nt):
        wz_recv(k).wait_recv()
        h = lax.rem(t + k, nt)
        for j in range(1, ny):
            wp_send(j, h).start()
        wp_sib(d, 0, h).start()

    def g_send(step, half):
        dev = across(step)[1]
        src, dst = (gsk, grk) if half else (gsq, grq)
        return remote(
            src.at[step - 1], dst.at[step - 1], g_s.at[step - 1, half], g_r.at[step - 1, half], dev
        )

    def sib_wait(n):
        for k in range(nc):
            p_wait(n, along(k)[0] + 1 - 2 * core)

    for step in range(1, ny):
        tok_wait(step)
    for n in range(own):
        sib_wait(n)
    for step in range(1, ny):

        @pl.loop(1, nx)
        def _(k):
            j = lax.rem(me + k, nx)
            gsq[step - 1] += q_terms(tokg[step, j], lambda p: dqp[j, p])

        g_send(step, 0).start()
    sib_wait(own)
    for step in range(1, ny):

        @pl.loop(1, nx)
        def _(k):
            j = lax.rem(me + k, nx)
            gsk[step - 1] += dot(tokg[step, j], dkvp[j], 0, 0)

        g_send(step, 1).start()

    for dist in range(2, nt - 1):
        for n in range(own + 1):
            z_pass(n, dist)

    for k in range(1, ny):
        j = across(k)[0]
        for i in range(1, nt):
            h = lax.rem(t + i, nt)
            w_wait(j, h)
            wp_sib(j, k, h).start()

    tok_wait(0)

    @pl.loop(1, nx)
    def _(k):
        j = lax.rem(me + k, nx)
        gw[:, :heads] += q_terms(tokg[0, j], lambda p: dqp[j, p])
        gw[:, heads:] += dot(tokg[0, j], dkvp[j], 0, 0)

    for k in range(ny):
        j = across(k)[0] + 1 - 2 * core
        for i in range(1, nt):
            w_wait(j, lax.rem(t + i, nt))
    for n in range(own + 1):
        z_pass(n, nt - 1)

    @pl.loop(1, nt)
    def _(k):
        h = lax.rem(t + k, nt)
        x_terms(h, lambda i: wg[h, i], False)

    gx[...] = gx_acc[...].astype(bf16)

    for step in range(1, ny):
        g_send(step, 0).wait_recv()
        gw[:, :heads] += grq[step - 1]
        g_send(step, 1).wait_recv()
        gw[:, heads:] += grk[step - 1]

    for k in range(1, nt):
        wz_send(k).wait_send()
    for step in range(ny):
        for k in range(1, nx):
            tok_send(step, k).wait_send()
    for k in range(1, nc):
        cls_send(k).wait_send()
        dcls_send(k).wait_send()
    for i in range(1, nt):
        h = lax.rem(t + i, nt)
        for k in range(1, ny):
            wp_send(k, h).wait_send()
            wp_sib(across(k)[0], k, h).wait_send()
        wp_sib(d, 0, h).wait_send()
    for n in range(own + 1):
        for side in (0, 1):
            to = t + 2 * side - 1

            @pl.when((to >= 0) & (to < nt))
            def _():
                z_copy(n, t, to, z_s.at[n, side]).wait_send()

            for dist in range(1, nt - 1):
                src, on = t + dist * (2 * side - 1), t - 2 * side + 1

                @pl.when((src >= 0) & (src < nt) & (on >= 0) & (on < nt))
                def _():
                    z_copy(n, src, on, zf_s.at[n, dist, side]).wait_send()

        for k in range(1, nc):
            p_send(n, k).wait_send()
            p_fwd(n, along(k)[0], k).wait_send()
        p_sib(n).wait_send()
    for step in range(1, ny):
        g_send(step, 0).wait_send()
        g_send(step, 1).wait_send()


def fused(sizes, tokens, qkv_weight, lengths, grad_out):
    nc, nt, nd, own, length = sizes
    ny, nx = nd // 2, nc * 2
    width, rows = tokens.shape[-1], own * length
    cols, xcols = width // (nc * nd), width // nt
    kv, heads = 2 * HD, GQ * HD
    dma = pltpu.SemaphoreType.DMA
    vmem = pl.BlockSpec(memory_space=pltpu.VMEM)
    flops = 6 * rows * width * (heads + kv)
    attended, grad_x, grad_w = pl.pallas_call(
        functools.partial(kernel, sizes),
        out_shape=(
            jax.ShapeDtypeStruct((rows, heads), bf16),
            jax.ShapeDtypeStruct((rows, xcols), bf16),
            jax.ShapeDtypeStruct((cols, heads + kv), f32),
        ),
        in_specs=[vmem, vmem, pl.BlockSpec(memory_space=pltpu.SMEM), vmem],
        out_specs=(vmem, vmem, vmem),
        scratch_shapes=[
            pltpu.VMEM((rows, heads), bf16),
            pltpu.VMEM((rows, kv), bf16),
            pltpu.VMEM((128, kv), bf16),
            pltpu.VMEM((128, kv), f32),
            pltpu.VMEM((nc, 16, kv), f32),
            pltpu.VMEM((rows, kv), f32),
            pltpu.VMEM((rows, xcols), f32),
            pltpu.VMEM((ny, nx, rows, cols), bf16),
            pltpu.VMEM((nt, nd, xcols // nd, heads + kv), bf16),
            pltpu.VMEM((nt, own, length, heads), bf16),
            pltpu.VMEM((nt, rows, kv), bf16),
            pltpu.VMEM((nx, own, length, heads), bf16),
            pltpu.VMEM((nx, rows, kv), bf16),
            pltpu.VMEM((ny - 1, cols, heads), f32),
            pltpu.VMEM((ny - 1, cols, kv), f32),
            pltpu.VMEM((ny - 1, cols, heads), f32),
            pltpu.VMEM((ny - 1, cols, kv), f32),
            dma((nc,)),
            dma((nc,)),
            dma((nc,)),
            dma((nc,)),
            dma((ny, nx)),
            dma((ny, nx)),
            dma((nt,)),
            dma((nt,)),
            dma((ny, nt)),
            dma((nd, nt)),
            dma((ny, nt)),
            dma((own + 1, 2)),
            dma((own + 1, nt)),
            dma((own + 1, nt, 2)),
            dma((own + 1, nc)),
            dma((own + 1, nx)),
            dma((own + 1, nc)),
            dma((ny - 1, 2)),
            dma((ny - 1, 2)),
        ],
        compiler_params=pltpu.CompilerParams(
            collective_id=0, has_side_effects=True, vmem_limit_bytes=58 * 2**20
        ),
        cost_estimate=pl.CostEstimate(
            flops=flops, bytes_accessed=16 * 2**20, transcendentals=rows * length * GQ
        ),
    )(
        tokens.reshape(rows, width),
        qkv_weight.reshape(width, heads + kv),
        lengths.reshape(own),
        grad_out.reshape(rows, heads),
    )
    return (
        attended.reshape(1, own, length, 1, heads),
        grad_x.reshape(1, own, length, xcols),
        grad_w.reshape(cols, 1, heads + kv),
    )


def local(sizes, tokens, qkv_weight, lengths, grad_out):
    nc, nt, nd = sizes
    lists, own, length, width = tokens.shape
    ne = nc * nd
    fits = (
        lists == 1
        and qkv_weight.shape[1] == 1
        and nd % 2 == 0
        and nd >= 4
        and nc >= 2
        and nt >= 3
        and nc * 16 <= 128
        and own <= 8
        and width % (ne * 128) == 0
        and width % (nd * nt * 128) == 0
        and length % 128 == 0
        and 2 * ne * own * length * (width // ne) <= 6 * 2**20
    )
    if fits:
        return fused((nc, nt, nd, own, length), tokens, qkv_weight, lengths, grad_out)
    return body(tokens, qkv_weight, lengths, grad_out)


def solution(mesh):
    placed = (
        P("dp", "cand", None, None),
        P(None, "tp", None),
        P("dp", "cand"),
        P("dp", "cand", None, "tp", None),
    )
    sizes = tuple(mesh.shape[name] for name in ("cand", "tp", "dp"))
    return jax.shard_map(
        functools.partial(local, sizes),
        mesh=mesh,
        in_specs=placed,
        out_specs=(
            P("dp", "cand", None, "tp", None),
            P("dp", "cand", None, "tp"),
            P(("cand", "dp"), "tp", None),
        ),
        check_vma=False,
    )
```

```python
import functools
import math

import jax
import jax.numpy as jnp
from jax import lax
from jax.experimental import pallas as pl
from jax.experimental.pallas import tpu as pltpu
from jax.sharding import PartitionSpec as P

GQ = 4
HD = 128


highest = lax.Precision.HIGHEST
masked_value = -1e30


def attend(queries, key_rows, value_rows, cls_keys, cls_values, lengths, first_index):
    head_size = queries.shape[-1]
    factor = 1.0 / math.sqrt(head_size)
    cand_total = queries.shape[0]
    seq_len = queries.shape[1]
    listed = cls_keys.shape[0]
    scores = jnp.einsum("clhge,cmhe->chglm", queries, key_rows, precision=highest) * factor
    visible = jnp.arange(seq_len)[None, :] < lengths[:, None]
    scores = jnp.where(visible[:, None, None, None, :], scores, masked_value)
    row_peak = lax.stop_gradient(jnp.max(scores, axis=-1, keepdims=True))
    weights = jnp.exp(scores - row_peak)
    totals = jnp.sum(weights, axis=-1)
    blended = jnp.einsum("chglm,cmhe->clhge", weights, value_rows, precision=highest)
    blended = blended / jnp.transpose(totals, (0, 3, 1, 2))[..., None]
    across = jnp.einsum("chge,ahe->chga", queries[:, 0], cls_keys, precision=highest) * factor
    own_slot = jnp.arange(listed)[None, :] == (first_index + jnp.arange(cand_total))[:, None]
    across = jnp.where(own_slot[:, None, None, :], masked_value, across)
    first_row = scores[:, :, :, 0, :]
    joint_peak = lax.stop_gradient(
        jnp.maximum(jnp.max(first_row, axis=-1), jnp.max(across, axis=-1))
    )[..., None]
    local_weights = jnp.exp(first_row - joint_peak)
    far_weights = jnp.exp(across - joint_peak)
    denominator = jnp.sum(local_weights, axis=-1) + jnp.sum(far_weights, axis=-1)
    head_row = jnp.einsum("chgm,cmhe->chge", local_weights, value_rows, precision=highest)
    head_row = head_row + jnp.einsum("chga,ahe->chge", far_weights, cls_values, precision=highest)
    head_row = head_row / denominator[..., None]
    return blended.at[:, 0].set(head_row)


def body(tokens, qkv_weight, lengths, grad_out):
    list_count, cand_count, seq_len, model_width = tokens.shape
    local_heads = qkv_weight.shape[1]
    row_count = list_count * cand_count * seq_len
    flat_rows = tokens.reshape(row_count, model_width)
    weight_mat = qkv_weight.reshape(model_width, -1)
    packed = jnp.dot(flat_rows, weight_mat, preferred_element_type=jnp.float32).astype(jnp.bfloat16)
    packed = packed.reshape(list_count, cand_count, seq_len, local_heads, (GQ + 2) * HD)
    query_part = packed[..., : GQ * HD].reshape(
        list_count, cand_count, seq_len, local_heads, GQ, HD
    )
    key_part = packed[..., GQ * HD : (GQ + 1) * HD]
    value_part = packed[..., (GQ + 1) * HD :]
    cls_keys, cls_values = (
        lax.all_gather(key_part[:, :, 0], "cand", axis=1, tiled=True),
        lax.all_gather(value_part[:, :, 0], "cand", axis=1, tiled=True),
    )
    first_index = lax.axis_index("cand") * cand_count

    def forward(q_in, k_in, v_in, ck_in, cv_in):
        return jax.vmap(attend, in_axes=(0, 0, 0, 0, 0, 0, None))(
            q_in, k_in, v_in, ck_in, cv_in, lengths, first_index
        )

    result, pullback = jax.vjp(
        forward,
        query_part.astype(jnp.float32),
        key_part.astype(jnp.float32),
        value_part.astype(jnp.float32),
        cls_keys.astype(jnp.float32),
        cls_values.astype(jnp.float32),
    )
    attended = result.reshape(list_count, cand_count, seq_len, local_heads, GQ * HD).astype(
        jnp.bfloat16
    )
    upstream = grad_out.astype(jnp.float32).reshape(
        list_count, cand_count, seq_len, local_heads, GQ, HD
    )
    d_query, d_key, d_value, d_cls_key, d_cls_value = pullback(upstream)
    own_key, own_value = (
        lax.psum_scatter(d_cls_key, "cand", scatter_dimension=1, tiled=True),
        lax.psum_scatter(d_cls_value, "cand", scatter_dimension=1, tiled=True),
    )
    d_key = d_key.at[:, :, 0].add(own_key)
    d_value = d_value.at[:, :, 0].add(own_value)
    d_packed = jnp.concatenate(
        [d_query.reshape(list_count, cand_count, seq_len, local_heads, GQ * HD), d_key, d_value],
        axis=-1,
    )
    d_packed = d_packed.astype(jnp.bfloat16).reshape(row_count, -1)
    partial_x = lax.dot_general(
        d_packed, weight_mat, (((1,), (1,)), ((), ())), preferred_element_type=jnp.float32
    )
    grad_x = lax.psum_scatter(partial_x, "tp", scatter_dimension=1, tiled=True).astype(jnp.bfloat16)
    grad_x = grad_x.reshape(list_count, cand_count, seq_len, -1)
    grad_w = lax.psum_scatter(
        lax.dot_general(
            flat_rows, d_packed, (((0,), (0,)), ((), ())), preferred_element_type=jnp.float32
        ),
        ("cand", "dp"),
        scatter_dimension=0,
        tiled=True,
    )
    return (attended, grad_x, grad_w.reshape(grad_w.shape[0], local_heads, -1))


MESH = pl.DeviceIdType.MESH
f32 = jnp.float32
bf16 = jnp.bfloat16


def dot(a, b, ca, cb):
    return lax.dot_general(a, b, (((ca,), (cb,)), ((), ())), preferred_element_type=f32)


def split(x):
    hi = x.astype(bf16)
    return hi, (x - hi.astype(f32)).astype(bf16)


def dot2(x, b, ca, cb):
    return dot(x[0], b, ca, cb) + dot(x[1], b, ca, cb)


def kernel(
    sizes,
    tok,
    w,
    lens,
    go,
    att,
    gx,
    gw,
    qb,
    kvb,
    cls,
    dcls,
    dclsr,
    dkv_acc,
    turned,
    gx_acc,
    tokg,
    wg,
    dqz,
    dkvz,
    dqp,
    dkvp,
    gsq,
    gsk,
    grq,
    grk,
    cls_s,
    cls_r,
    dcls_s,
    dcls_r,
    tok_s,
    tok_r,
    wz_s,
    wz_r,
    wp_s,
    wp_r,
    wf_s,
    z_s,
    z_r,
    zf_s,
    p_s,
    p_r,
    pf_s,
    g_s,
    g_r,
):
    nc, nt, nd, own, length = sizes
    ny, nx = nd // 2, nc * 2
    c, t, d = lax.axis_index("cand"), lax.axis_index("tp"), lax.axis_index("dp")
    y, core = d // 2, lax.rem(d, 2)
    sib = d + 1 - 2 * core
    me = c * 2 + core
    cols = tok.shape[1] // (nc * nd)
    xcols = w.shape[0] // nt
    part = xcols // nd
    heads = GQ * HD
    scale = 1.0 / math.sqrt(HD)

    cls[...] = jnp.zeros_like(cls)
    dcls[...] = jnp.zeros_like(dcls)

    def row(k):
        j = lax.rem(me + k, nx)
        return j, {"cand": j // 2, "dp": 2 * y + lax.rem(j, 2)}

    def along(k):
        j = lax.rem(c + k, nc)
        return j * 2 + core, {"cand": j}

    def across(k):
        j = 2 * lax.rem(y + k, ny) + core
        return j, {"dp": j}

    barrier = pltpu.get_barrier_semaphore()
    for k in range(1, nx):
        pl.semaphore_signal(barrier, inc=1, device_id=row(k)[1], device_id_type=MESH)
    for k in range(1, ny):
        pl.semaphore_signal(barrier, inc=1, device_id=across(k)[1], device_id_type=MESH)
    for k in range(1, nt):
        pl.semaphore_signal(
            barrier, inc=1, device_id={"tp": lax.rem(t + k, nt)}, device_id_type=MESH
        )
    pl.semaphore_wait(barrier, nx - 1 + ny - 1 + nt - 1)

    def remote(src, dst, ss, rs, dev):
        return pltpu.make_async_remote_copy(
            src_ref=src, dst_ref=dst, send_sem=ss, recv_sem=rs, device_id=dev, device_id_type=MESH
        )

    def wz_send(k):
        o = lax.rem(t + k, nt)
        return remote(
            w.at[pl.ds(pl.multiple_of(o * xcols + d * part, 16), part)],
            wg.at[t, d],
            wz_s.at[k],
            wz_r.at[t],
            {"tp": o},
        )

    def wz_recv(k):
        h = lax.rem(t + k, nt)
        return remote(wg.at[h, d], wg.at[h, d], wz_s.at[k], wz_r.at[h], {"tp": h})

    def wp_send(k, h):
        return remote(wg.at[h, d], wg.at[h, d], wp_s.at[k, h], wp_r.at[d, h], across(k)[1])

    def wp_sib(j, k, h):
        return remote(wg.at[h, j], wg.at[h, j], wf_s.at[k, h], wp_r.at[j, h], {"dp": sib})

    def w_wait(j, h):
        remote(wg.at[h, j], wg.at[h, j], wf_s.at[0, h], wp_r.at[j, h], {"dp": sib}).wait_recv()

    def block(cc, step, kk):
        j = cc * nd + 2 * lax.rem(y + step, ny) + kk
        return pl.ds(pl.multiple_of(j * cols, 128), cols)

    def tok_send(step, k):
        j, dev = row(k)
        return remote(
            tok.at[:, block(j // 2, step, lax.rem(j, 2))],
            tokg.at[step, me],
            tok_s.at[step, k],
            tok_r.at[step, me],
            dev,
        )

    def tok_wait(step):
        for k in range(1, nx):
            j, dev = row(k)
            remote(
                tokg.at[step, j], tokg.at[step, j], tok_s.at[step, k], tok_r.at[step, j], dev
            ).wait_recv()

    for k in range(1, nt):
        wz_send(k).start()
    for step in range(1, ny):
        for k in range(1, nx):
            tok_send(step, k).start()

    def zbuf(n, s):
        return dqz.at[s, n] if n < own else dkvz.at[s]

    def pbuf(n, s):
        return dqp.at[s, n] if n < own else dkvp.at[s]

    def z_copy(n, s, to, ss):
        return remote(zbuf(n, s), zbuf(n, s), ss, z_r.at[n, s], {"tp": to})

    def p_send(n, k):
        return remote(zbuf(n, t), pbuf(n, me), p_s.at[n, k], p_r.at[n, me], along(k)[1])

    def p_sib(n):
        return remote(zbuf(n, t), pbuf(n, me), pf_s.at[n, 0], p_r.at[n, me], {"dp": sib})

    def p_fwd(n, j, k):
        return remote(pbuf(n, j), pbuf(n, j), pf_s.at[n, k], p_r.at[n, j], {"dp": sib})

    def p_wait(n, j):
        remote(pbuf(n, j), pbuf(n, j), pf_s.at[n, 0], p_r.at[n, j], {"dp": sib}).wait_recv()

    def send_chunk(n):
        for side in (0, 1):
            to = t + 2 * side - 1

            @pl.when((to >= 0) & (to < nt))
            def _():
                z_copy(n, t, to, z_s.at[n, side]).start()

        for k in range(1, nc):
            p_send(n, k).start()
        p_sib(n).start()

    kvb[...] = dot(tok[...], w[:, heads:], 1, 0).astype(bf16)
    first = lax.broadcasted_iota(jnp.int32, (16, 2 * HD), 0)
    mine = jnp.zeros((16, 2 * HD), f32)
    for p in range(own):
        cls_row = kvb[p * length : p * length + 16, :].astype(f32)[0:1]
        mine = jnp.where(first == p, cls_row, mine)

    def rows_of(j):
        return pl.ds(pl.multiple_of(j * 16, 16), 16)

    cls[rows_of(c), :] = mine.astype(bf16)

    def cls_send(k):
        return remote(
            cls.at[rows_of(c)], cls.at[rows_of(c)], cls_s.at[k], cls_r.at[c], along(k)[1]
        )

    def cls_recv(k):
        o = lax.rem(c + k, nc)
        return remote(cls.at[rows_of(o)], cls.at[rows_of(o)], cls_s.at[k], cls_r.at[o], {"cand": o})

    def dcls_send(k):
        o = lax.rem(c + k, nc)
        return remote(dcls.at[rows_of(o)], dclsr.at[c], dcls_s.at[k], dcls_r.at[c], {"cand": o})

    for k in range(1, nc):
        cls_send(k).start()

    @pl.loop(0, heads // 256)
    def _(i):
        at = pl.ds(pl.multiple_of(i * 256, 256), 256)
        qb[:, at] = dot(tok[...], w[:, at], 1, 0).astype(bf16)

    for k in range(1, nc):
        cls_recv(k).wait_recv()

    far_lane = lax.broadcasted_iota(jnp.int32, (16, 128), 1)
    far_row = lax.broadcasted_iota(jnp.int32, (16, 128), 0)
    lane = lax.broadcasted_iota(jnp.int32, (length, length), 1)

    for p in range(own):
        at = slice(p * length, (p + 1) * length)
        visible = lane < lens[p]
        listed = (far_row == 0) & (lax.rem(far_lane, 16) < own) & (far_lane < nc * 16)
        listed = listed & (far_lane != c * 16 + p)

        turned[...] = jnp.zeros_like(turned)

        @pl.loop(0, GQ, unroll=2)
        def _(g):
            head = pl.ds(pl.multiple_of(g * HD, HD), HD)
            q, do = qb[at, head], go[at, head]
            k, v = kvb[at, :HD], kvb[at, HD:]
            ck, cv = cls[:, :HD], cls[:, HD:]
            q16, do16 = q[:16], do[:16]
            s = jnp.where(visible, dot(q, k, 1, 1), masked_value)
            f = jnp.where(listed, dot(q16, ck, 1, 1), masked_value)
            m = jnp.max(s, axis=1, keepdims=True)
            m16 = jnp.maximum(m[:16], jnp.max(f, axis=1, keepdims=True))
            m = jnp.concatenate([m16, m[16:]], axis=0)
            pr, pf = jnp.exp((s - m) * scale), jnp.exp((f - m16) * scale)
            total = jnp.sum(pr, axis=1, keepdims=True)
            t16 = total[:16] + jnp.sum(pf, axis=1, keepdims=True)
            total = jnp.concatenate([t16, total[16:]], axis=0)
            over = 1.0 / total
            pr, pf = pr * over, pf * over[:16]
            prs, pfs = split(pr), split(pf)
            o = dot2(prs, v, 1, 0)
            o = jnp.concatenate([o[:16] + dot2(pfs, cv, 1, 0), o[16:]], axis=0)
            att[at, head] = o.astype(bf16)
            delta = jnp.sum(o * do.astype(f32), axis=1, keepdims=True)
            ds = split(pr * (dot(do, v, 1, 1) - delta))
            dsf = split(pf * (dot(do16, cv, 1, 1) - delta[:16]) * scale)
            dq = dot2(ds, k, 1, 0) * scale
            dq = jnp.concatenate([dq[:16] + dot2(dsf, ck, 1, 0), dq[16:]], axis=0)
            dqz[t, p, :, head] = dq.astype(bf16)
            turned[:HD, :] += dot(q, ds[0], 0, 0) + dot(q, ds[1], 0, 0)
            turned[HD:, :] += dot(do, prs[0], 0, 0) + dot(do, prs[1], 0, 0)
            dcls[:, :HD] += dot2(dsf, q16, 0, 0)
            dcls[:, HD:] += dot2(pfs, do16, 0, 0)

        dkv_acc[at, :HD] = turned[:HD, :].T * scale
        dkv_acc[at, HD:] = turned[HD:, :].T
        if p == own - 1:
            for k in range(1, nc):
                dcls_send(k).start()
        send_chunk(p)

    mine = dcls[rows_of(c), :]
    for k in range(1, nc):
        o = lax.rem(c + k, nc)
        remote(dclsr.at[o], dclsr.at[o], dcls_s.at[k], dcls_r.at[o], {"cand": o}).wait_recv()
        mine = mine + dclsr[o]
    top = lax.broadcasted_iota(jnp.int32, (8, 2 * HD), 0)
    for p in range(own):
        at = slice(p * length, p * length + 8)
        dkv_acc[at, :] = dkv_acc[at, :] + jnp.where(top == 0, mine[p : p + 1], 0.0)
    dkvz[t] = dkv_acc[...].astype(bf16)
    send_chunk(own)
    for k in range(1, nx):
        tok_send(0, k).start()

    def x_terms(h, weight, start):
        @pl.loop(0, nd)
        def _(i):
            wi = weight(i)
            at = pl.ds(pl.multiple_of(i * part, 128), part)
            for p in range(own):
                rs = slice(p * length, (p + 1) * length)
                v = dot(dqz[h, p], wi[:, :heads], 1, 1)
                v = v + dot(dkvz[h, rs, :], wi[:, heads:], 1, 1)
                if start:
                    gx_acc[rs, at] = v
                else:
                    gx_acc[rs, at] += v

    def q_terms(x, dq):
        v = dot(x[:length], dq(0), 0, 0)
        for p in range(1, own):
            v = v + dot(x[p * length : (p + 1) * length], dq(p), 0, 0)
        return v

    def own_cols(step):
        return tok[:, block(c, step, core)]

    x_terms(t, lambda i: w[pl.ds(pl.multiple_of(t * xcols + i * part, 16), part), :], True)
    for k in range(1, nt):
        wz_recv(k).wait_recv()
        h = lax.rem(t + k, nt)
        for j in range(1, ny):
            wp_send(j, h).start()
        wp_sib(d, 0, h).start()

    for step in range(1, ny):
        x = own_cols(step)
        gsq[step - 1] = q_terms(x, lambda p: dqz[t, p])
        gsk[step - 1] = dot(x, dkvz[t], 0, 0)
    x = own_cols(0)
    gw[:, :heads] = q_terms(x, lambda p: dqz[t, p])
    gw[:, heads:] = dot(x, dkvz[t], 0, 0)

    def z_pass(n, dist):
        for side in (0, 1):
            src, to = t + dist * (2 * side - 1), t - 2 * side + 1

            @pl.when((src >= 0) & (src < nt))
            def _():
                z_copy(n, src, t, zf_s.at[n, dist, side]).wait_recv()
                if dist < nt - 1:

                    @pl.when((to >= 0) & (to < nt))
                    def _():
                        z_copy(n, src, to, zf_s.at[n, dist, side]).start()

    for n in range(own + 1):
        z_pass(n, 1)
        for k in range(1, nc):
            j = along(k)[0]
            p_wait(n, j)
            p_fwd(n, j, k).start()
    def g_send(step, half):
        dev = across(step)[1]
        src, dst = (gsk, grk) if half else (gsq, grq)
        return remote(
            src.at[step - 1], dst.at[step - 1], g_s.at[step - 1, half], g_r.at[step - 1, half], dev
        )

    def sib_wait(n):
        for k in range(nc):
            p_wait(n, along(k)[0] + 1 - 2 * core)

    for step in range(1, ny):
        tok_wait(step)
    for n in range(own):
        sib_wait(n)
    for step in range(1, ny):

        @pl.loop(1, nx)
        def _(k):
            j = lax.rem(me + k, nx)
            gsq[step - 1] += q_terms(tokg[step, j], lambda p: dqp[j, p])

        g_send(step, 0).start()
    sib_wait(own)
    for step in range(1, ny):

        @pl.loop(1, nx)
        def _(k):
            j = lax.rem(me + k, nx)
            gsk[step - 1] += dot(tokg[step, j], dkvp[j], 0, 0)

        g_send(step, 1).start()

    for dist in range(2, nt - 1):
        for n in range(own + 1):
            z_pass(n, dist)

    for k in range(1, ny):
        j = across(k)[0]
        for i in range(1, nt):
            h = lax.rem(t + i, nt)
            w_wait(j, h)
            wp_sib(j, k, h).start()

    tok_wait(0)

    @pl.loop(1, nx)
    def _(k):
        j = lax.rem(me + k, nx)
        gw[:, :heads] += q_terms(tokg[0, j], lambda p: dqp[j, p])
        gw[:, heads:] += dot(tokg[0, j], dkvp[j], 0, 0)

    for k in range(ny):
        j = across(k)[0] + 1 - 2 * core
        for i in range(1, nt):
            w_wait(j, lax.rem(t + i, nt))
    for dist in range(1, nt):
        if dist == nt - 1:
            for n in range(own + 1):
                z_pass(n, dist)
        for side in (0, 1):
            src = t + dist * (2 * side - 1)

            @pl.when((src >= 0) & (src < nt))
            def _():
                x_terms(src, lambda i: wg[src, i], False)

    gx[...] = gx_acc[...].astype(bf16)

    for step in range(1, ny):
        g_send(step, 0).wait_recv()
        gw[:, :heads] += grq[step - 1]
        g_send(step, 1).wait_recv()
        gw[:, heads:] += grk[step - 1]

    for k in range(1, nt):
        wz_send(k).wait_send()
    for step in range(ny):
        for k in range(1, nx):
            tok_send(step, k).wait_send()
    for k in range(1, nc):
        cls_send(k).wait_send()
        dcls_send(k).wait_send()
    for i in range(1, nt):
        h = lax.rem(t + i, nt)
        for k in range(1, ny):
            wp_send(k, h).wait_send()
            wp_sib(across(k)[0], k, h).wait_send()
        wp_sib(d, 0, h).wait_send()
    for n in range(own + 1):
        for side in (0, 1):
            to = t + 2 * side - 1

            @pl.when((to >= 0) & (to < nt))
            def _():
                z_copy(n, t, to, z_s.at[n, side]).wait_send()

            for dist in range(1, nt - 1):
                src, on = t + dist * (2 * side - 1), t - 2 * side + 1

                @pl.when((src >= 0) & (src < nt) & (on >= 0) & (on < nt))
                def _():
                    z_copy(n, src, on, zf_s.at[n, dist, side]).wait_send()

        for k in range(1, nc):
            p_send(n, k).wait_send()
            p_fwd(n, along(k)[0], k).wait_send()
        p_sib(n).wait_send()
    for step in range(1, ny):
        g_send(step, 0).wait_send()
        g_send(step, 1).wait_send()


def fused(sizes, tokens, qkv_weight, lengths, grad_out):
    nc, nt, nd, own, length = sizes
    ny, nx = nd // 2, nc * 2
    width, rows = tokens.shape[-1], own * length
    cols, xcols = width // (nc * nd), width // nt
    kv, heads = 2 * HD, GQ * HD
    dma = pltpu.SemaphoreType.DMA
    vmem = pl.BlockSpec(memory_space=pltpu.VMEM)
    flops = 6 * rows * width * (heads + kv)
    attended, grad_x, grad_w = pl.pallas_call(
        functools.partial(kernel, sizes),
        out_shape=(
            jax.ShapeDtypeStruct((rows, heads), bf16),
            jax.ShapeDtypeStruct((rows, xcols), bf16),
            jax.ShapeDtypeStruct((cols, heads + kv), f32),
        ),
        in_specs=[vmem, vmem, pl.BlockSpec(memory_space=pltpu.SMEM), vmem],
        out_specs=(vmem, vmem, vmem),
        scratch_shapes=[
            pltpu.VMEM((rows, heads), bf16),
            pltpu.VMEM((rows, kv), bf16),
            pltpu.VMEM((128, kv), bf16),
            pltpu.VMEM((128, kv), f32),
            pltpu.VMEM((nc, 16, kv), f32),
            pltpu.VMEM((rows, kv), f32),
            pltpu.VMEM((kv, length), f32),
            pltpu.VMEM((rows, xcols), f32),
            pltpu.VMEM((ny, nx, rows, cols), bf16),
            pltpu.VMEM((nt, nd, xcols // nd, heads + kv), bf16),
            pltpu.VMEM((nt, own, length, heads), bf16),
            pltpu.VMEM((nt, rows, kv), bf16),
            pltpu.VMEM((nx, own, length, heads), bf16),
            pltpu.VMEM((nx, rows, kv), bf16),
            pltpu.VMEM((ny - 1, cols, heads), f32),
            pltpu.VMEM((ny - 1, cols, kv), f32),
            pltpu.VMEM((ny - 1, cols, heads), f32),
            pltpu.VMEM((ny - 1, cols, kv), f32),
            dma((nc,)),
            dma((nc,)),
            dma((nc,)),
            dma((nc,)),
            dma((ny, nx)),
            dma((ny, nx)),
            dma((nt,)),
            dma((nt,)),
            dma((ny, nt)),
            dma((nd, nt)),
            dma((ny, nt)),
            dma((own + 1, 2)),
            dma((own + 1, nt)),
            dma((own + 1, nt, 2)),
            dma((own + 1, nc)),
            dma((own + 1, nx)),
            dma((own + 1, nc)),
            dma((ny - 1, 2)),
            dma((ny - 1, 2)),
        ],
        compiler_params=pltpu.CompilerParams(
            collective_id=0, has_side_effects=True, vmem_limit_bytes=58 * 2**20
        ),
        cost_estimate=pl.CostEstimate(
            flops=flops, bytes_accessed=16 * 2**20, transcendentals=rows * length * GQ
        ),
    )(
        tokens.reshape(rows, width),
        qkv_weight.reshape(width, heads + kv),
        lengths.reshape(own),
        grad_out.reshape(rows, heads),
    )
    return (
        attended.reshape(1, own, length, 1, heads),
        grad_x.reshape(1, own, length, xcols),
        grad_w.reshape(cols, 1, heads + kv),
    )


def local(sizes, tokens, qkv_weight, lengths, grad_out):
    nc, nt, nd = sizes
    lists, own, length, width = tokens.shape
    ne = nc * nd
    fits = (
        lists == 1
        and qkv_weight.shape[1] == 1
        and nd % 2 == 0
        and nd >= 4
        and nc >= 2
        and nt >= 3
        and nc * 16 <= 128
        and own <= 8
        and width % (ne * 128) == 0
        and width % (nd * nt * 128) == 0
        and length % 128 == 0
        and 2 * ne * own * length * (width // ne) <= 6 * 2**20
    )
    if fits:
        return fused((nc, nt, nd, own, length), tokens, qkv_weight, lengths, grad_out)
    return body(tokens, qkv_weight, lengths, grad_out)


def solution(mesh):
    placed = (
        P("dp", "cand", None, None),
        P(None, "tp", None),
        P("dp", "cand"),
        P("dp", "cand", None, "tp", None),
    )
    sizes = tuple(mesh.shape[name] for name in ("cand", "tp", "dp"))
    return jax.shard_map(
        functools.partial(local, sizes),
        mesh=mesh,
        in_specs=placed,
        out_specs=(
            P("dp", "cand", None, "tp", None),
            P("dp", "cand", None, "tp"),
            P(("cand", "dp"), "tp", None),
        ),
        check_vma=False,
    )
```

```python
import functools
import math

import jax
import jax.numpy as jnp
from jax import lax
from jax.experimental import pallas as pl
from jax.experimental.pallas import tpu as pltpu
from jax.sharding import PartitionSpec as P

GQ = 4
HD = 128


highest = lax.Precision.HIGHEST
masked_value = -1e30


def attend(queries, key_rows, value_rows, cls_keys, cls_values, lengths, first_index):
    head_size = queries.shape[-1]
    factor = 1.0 / math.sqrt(head_size)
    cand_total = queries.shape[0]
    seq_len = queries.shape[1]
    listed = cls_keys.shape[0]
    scores = jnp.einsum("clhge,cmhe->chglm", queries, key_rows, precision=highest) * factor
    visible = jnp.arange(seq_len)[None, :] < lengths[:, None]
    scores = jnp.where(visible[:, None, None, None, :], scores, masked_value)
    row_peak = lax.stop_gradient(jnp.max(scores, axis=-1, keepdims=True))
    weights = jnp.exp(scores - row_peak)
    totals = jnp.sum(weights, axis=-1)
    blended = jnp.einsum("chglm,cmhe->clhge", weights, value_rows, precision=highest)
    blended = blended / jnp.transpose(totals, (0, 3, 1, 2))[..., None]
    across = jnp.einsum("chge,ahe->chga", queries[:, 0], cls_keys, precision=highest) * factor
    own_slot = jnp.arange(listed)[None, :] == (first_index + jnp.arange(cand_total))[:, None]
    across = jnp.where(own_slot[:, None, None, :], masked_value, across)
    first_row = scores[:, :, :, 0, :]
    joint_peak = lax.stop_gradient(
        jnp.maximum(jnp.max(first_row, axis=-1), jnp.max(across, axis=-1))
    )[..., None]
    local_weights = jnp.exp(first_row - joint_peak)
    far_weights = jnp.exp(across - joint_peak)
    denominator = jnp.sum(local_weights, axis=-1) + jnp.sum(far_weights, axis=-1)
    head_row = jnp.einsum("chgm,cmhe->chge", local_weights, value_rows, precision=highest)
    head_row = head_row + jnp.einsum("chga,ahe->chge", far_weights, cls_values, precision=highest)
    head_row = head_row / denominator[..., None]
    return blended.at[:, 0].set(head_row)


def body(tokens, qkv_weight, lengths, grad_out):
    list_count, cand_count, seq_len, model_width = tokens.shape
    local_heads = qkv_weight.shape[1]
    row_count = list_count * cand_count * seq_len
    flat_rows = tokens.reshape(row_count, model_width)
    weight_mat = qkv_weight.reshape(model_width, -1)
    packed = jnp.dot(flat_rows, weight_mat, preferred_element_type=jnp.float32).astype(jnp.bfloat16)
    packed = packed.reshape(list_count, cand_count, seq_len, local_heads, (GQ + 2) * HD)
    query_part = packed[..., : GQ * HD].reshape(
        list_count, cand_count, seq_len, local_heads, GQ, HD
    )
    key_part = packed[..., GQ * HD : (GQ + 1) * HD]
    value_part = packed[..., (GQ + 1) * HD :]
    cls_keys, cls_values = (
        lax.all_gather(key_part[:, :, 0], "cand", axis=1, tiled=True),
        lax.all_gather(value_part[:, :, 0], "cand", axis=1, tiled=True),
    )
    first_index = lax.axis_index("cand") * cand_count

    def forward(q_in, k_in, v_in, ck_in, cv_in):
        return jax.vmap(attend, in_axes=(0, 0, 0, 0, 0, 0, None))(
            q_in, k_in, v_in, ck_in, cv_in, lengths, first_index
        )

    result, pullback = jax.vjp(
        forward,
        query_part.astype(jnp.float32),
        key_part.astype(jnp.float32),
        value_part.astype(jnp.float32),
        cls_keys.astype(jnp.float32),
        cls_values.astype(jnp.float32),
    )
    attended = result.reshape(list_count, cand_count, seq_len, local_heads, GQ * HD).astype(
        jnp.bfloat16
    )
    upstream = grad_out.astype(jnp.float32).reshape(
        list_count, cand_count, seq_len, local_heads, GQ, HD
    )
    d_query, d_key, d_value, d_cls_key, d_cls_value = pullback(upstream)
    own_key, own_value = (
        lax.psum_scatter(d_cls_key, "cand", scatter_dimension=1, tiled=True),
        lax.psum_scatter(d_cls_value, "cand", scatter_dimension=1, tiled=True),
    )
    d_key = d_key.at[:, :, 0].add(own_key)
    d_value = d_value.at[:, :, 0].add(own_value)
    d_packed = jnp.concatenate(
        [d_query.reshape(list_count, cand_count, seq_len, local_heads, GQ * HD), d_key, d_value],
        axis=-1,
    )
    d_packed = d_packed.astype(jnp.bfloat16).reshape(row_count, -1)
    partial_x = lax.dot_general(
        d_packed, weight_mat, (((1,), (1,)), ((), ())), preferred_element_type=jnp.float32
    )
    grad_x = lax.psum_scatter(partial_x, "tp", scatter_dimension=1, tiled=True).astype(jnp.bfloat16)
    grad_x = grad_x.reshape(list_count, cand_count, seq_len, -1)
    grad_w = lax.psum_scatter(
        lax.dot_general(
            flat_rows, d_packed, (((0,), (0,)), ((), ())), preferred_element_type=jnp.float32
        ),
        ("cand", "dp"),
        scatter_dimension=0,
        tiled=True,
    )
    return (attended, grad_x, grad_w.reshape(grad_w.shape[0], local_heads, -1))


MESH = pl.DeviceIdType.MESH
f32 = jnp.float32
bf16 = jnp.bfloat16


def dot(a, b, ca, cb):
    return lax.dot_general(a, b, (((ca,), (cb,)), ((), ())), preferred_element_type=f32)


def split(x):
    hi = x.astype(bf16)
    return hi, (x - hi.astype(f32)).astype(bf16)


def dot2(x, b, ca, cb):
    return dot(x[0], b, ca, cb) + dot(x[1], b, ca, cb)


def kernel(
    sizes,
    tok,
    w,
    lens,
    go,
    att,
    gx,
    gw,
    qb,
    kvb,
    cls,
    dcls,
    dclsr,
    dkv_acc,
    turned,
    gx_acc,
    tokg,
    wg,
    dqz,
    dkvz,
    dqp,
    dkvp,
    gsq,
    gsk,
    grq,
    grk,
    gw_acc,
    cls_s,
    cls_r,
    dcls_s,
    dcls_r,
    tok_s,
    tok_r,
    wz_s,
    wz_r,
    wp_s,
    wp_r,
    z_s,
    z_r,
    zf_s,
    p_s,
    p_r,
    g_s,
    g_r,
):
    nc, nt, nd, own, length = sizes
    c, t, d = lax.axis_index("cand"), lax.axis_index("tp"), lax.axis_index("dp")
    y, core = d // 2, lax.rem(d, 2)
    cols = tok.shape[1] // (nc * nd)
    xcols = w.shape[0] // nt
    part = xcols // (nc * nd)
    heads = GQ * HD
    scale = 1.0 / math.sqrt(HD)

    cls[...] = jnp.zeros_like(cls)
    dcls[...] = jnp.zeros_like(dcls)

    def at_x(kk):
        return {"cand": 1 - c, "dp": 2 * y + kk}

    def at_y(kk):
        return {"cand": c, "dp": 2 * (1 - y) + kk}

    def index(dev):
        return dev["cand"] * nd + dev["dp"]

    flip = 1 - core
    sib = {"cand": c, "dp": 2 * y + flip}
    gather = {"cand": c * core + (1 - c) * flip, "dp": 2 * (y * flip + (1 - y) * core) + core}
    add = {"cand": c * flip + (1 - c) * core, "dp": 2 * (y * core + (1 - y) * flip) + core}
    e, e_sib, e_gather, e_add = c * nd + d, index(sib), index(gather), index(add)
    e_far = (1 - c) * nd + 2 * (1 - y) + core
    sib_add = (c * core + (1 - c) * flip) * nd + 2 * (y * flip + (1 - y) * core) + flip
    users = (
        (sib, 0, (e_sib, sib_add)),
        (at_x(0), 1 + core, (index(at_x(0)), (1 - c) * nd + 2 * (1 - y))),
        (at_y(1), 1 + core, (index(at_y(1)), (1 - c) * nd + 2 * (1 - y) + 1)),
    )

    barrier = pltpu.get_barrier_semaphore()
    for dev in (sib, at_x(0), at_x(1), at_y(0), at_y(1)):
        pl.semaphore_signal(barrier, inc=1, device_id=dev, device_id_type=MESH)
    for k in range(1, nt):
        pl.semaphore_signal(
            barrier, inc=1, device_id={"tp": lax.rem(t + k, nt)}, device_id_type=MESH
        )
    pl.semaphore_wait(barrier, 5 + nt - 1)

    def remote(src, dst, ss, rs, dev):
        return pltpu.make_async_remote_copy(
            src_ref=src, dst_ref=dst, send_sem=ss, recv_sem=rs, device_id=dev, device_id_type=MESH
        )

    def wz_send(k):
        o = lax.rem(t + k, nt)
        return remote(
            w.at[pl.ds(pl.multiple_of(o * xcols + e * part, 16), part)],
            wg.at[t, e],
            wz_s.at[k],
            wz_r.at[t],
            {"tp": o},
        )

    def wz_recv(k):
        h = lax.rem(t + k, nt)
        return remote(wg.at[h, e], wg.at[h, e], wz_s.at[k], wz_r.at[h], {"tp": h})

    def wp(k, j, h, dev):
        return remote(wg.at[h, j], wg.at[h, j], wp_s.at[k, h], wp_r.at[j, h], dev)

    w_first = ((0, e, at_x(core)), (1, e, at_y(core)), (2, e, sib))
    w_second = ((3, e_gather, add), (4, e_gather, sib), (5, e_add, sib))
    w_third = ((6, e_far, sib),)

    def w_start(copies):
        for i in range(1, nt):
            for k, j, dev in copies:
                wp(k, j, lax.rem(t + i, nt), dev).start()

    def w_wait(slots):
        for i in range(1, nt):
            for j in slots:
                wp(0, j, lax.rem(t + i, nt), sib).wait_recv()

    def block(j):
        return pl.ds(pl.multiple_of(j * cols, 128), cols)

    def tok_send(step, k):
        dev, slot, blocks = users[k]
        return remote(
            tok.at[:, block(blocks[step])],
            tokg.at[step, slot],
            tok_s.at[step, k],
            tok_r.at[step, slot],
            dev,
        )

    def tok_wait(step):
        for k in range(3):
            remote(
                tokg.at[step, k], tokg.at[step, k], tok_s.at[step, k], tok_r.at[step, k], sib
            ).wait_recv()

    for k in range(1, nt):
        wz_send(k).start()
    for step in (1, 0):
        for k in range(3):
            tok_send(step, k).start()

    def zbuf(n, s):
        return dqz.at[s, n] if n < own else dkvz.at[s]

    def pbuf(n, s):
        return dqp.at[s, n] if n < own else dkvp.at[s]

    def z_copy(n, s, to, ss):
        return remote(zbuf(n, s), zbuf(n, s), ss, z_r.at[n, s], {"tp": to})

    def p_send(n, k):
        dev, slot, _ = users[k]
        return remote(zbuf(n, t), pbuf(n, slot), p_s.at[n, k], p_r.at[n, slot], dev)

    def p_wait(n):
        for k in range(3):
            remote(pbuf(n, k), pbuf(n, k), p_s.at[n, k], p_r.at[n, k], sib).wait_recv()

    def send_chunk(n):
        for side in (0, 1):
            to = t + 2 * side - 1

            @pl.when((to >= 0) & (to < nt))
            def _():
                z_copy(n, t, to, z_s.at[n, side]).start()

        for k in range(3):
            p_send(n, k).start()

    kvb[...] = dot(tok[...], w[:, heads:], 1, 0).astype(bf16)
    first = lax.broadcasted_iota(jnp.int32, (16, 2 * HD), 0)
    mine = jnp.zeros((16, 2 * HD), f32)
    for p in range(own):
        cls_row = kvb[p * length : p * length + 16, :].astype(f32)[0:1]
        mine = jnp.where(first == p, cls_row, mine)

    def rows_of(j):
        return pl.ds(pl.multiple_of(j * 16, 16), 16)

    cls[rows_of(c), :] = mine.astype(bf16)

    def cls_send(k):
        return remote(
            cls.at[rows_of(c)], cls.at[rows_of(c)], cls_s.at[k], cls_r.at[c], {"cand": lax.rem(c + k, nc)}
        )

    def cls_recv(k):
        o = lax.rem(c + k, nc)
        return remote(cls.at[rows_of(o)], cls.at[rows_of(o)], cls_s.at[k], cls_r.at[o], {"cand": o})

    def dcls_send(k):
        o = lax.rem(c + k, nc)
        return remote(dcls.at[rows_of(o)], dclsr.at[c], dcls_s.at[k], dcls_r.at[c], {"cand": o})

    for k in range(1, nc):
        cls_send(k).start()

    @pl.loop(0, heads // 256)
    def _(i):
        at = pl.ds(pl.multiple_of(i * 256, 256), 256)
        qb[:, at] = dot(tok[...], w[:, at], 1, 0).astype(bf16)

    for k in range(1, nc):
        cls_recv(k).wait_recv()

    far_lane = lax.broadcasted_iota(jnp.int32, (16, 128), 1)
    far_row = lax.broadcasted_iota(jnp.int32, (16, 128), 0)
    lane = lax.broadcasted_iota(jnp.int32, (length, length), 1)

    for p in range(own):
        at = slice(p * length, (p + 1) * length)
        visible = lane < lens[p]
        listed = (far_row == 0) & (lax.rem(far_lane, 16) < own) & (far_lane < nc * 16)
        listed = listed & (far_lane != c * 16 + p)

        turned[...] = jnp.zeros_like(turned)

        @pl.loop(0, GQ, unroll=2)
        def _(g):
            head = pl.ds(pl.multiple_of(g * HD, HD), HD)
            q, do = qb[at, head], go[at, head]
            k, v = kvb[at, :HD], kvb[at, HD:]
            ck, cv = cls[:, :HD], cls[:, HD:]
            q16, do16 = q[:16], do[:16]
            s = jnp.where(visible, dot(q, k, 1, 1), masked_value)
            f = jnp.where(listed, dot(q16, ck, 1, 1), masked_value)
            m = jnp.max(s, axis=1, keepdims=True)
            m16 = jnp.maximum(m[:16], jnp.max(f, axis=1, keepdims=True))
            m = jnp.concatenate([m16, m[16:]], axis=0)
            pr, pf = jnp.exp((s - m) * scale), jnp.exp((f - m16) * scale)
            total = jnp.sum(pr, axis=1, keepdims=True)
            t16 = total[:16] + jnp.sum(pf, axis=1, keepdims=True)
            total = jnp.concatenate([t16, total[16:]], axis=0)
            over = 1.0 / total
            pr, pf = pr * over, pf * over[:16]
            prs, pfs = split(pr), split(pf)
            o = dot2(prs, v, 1, 0)
            o = jnp.concatenate([o[:16] + dot2(pfs, cv, 1, 0), o[16:]], axis=0)
            att[at, head] = o.astype(bf16)
            delta = jnp.sum(o * do.astype(f32), axis=1, keepdims=True)
            ds = split(pr * (dot(do, v, 1, 1) - delta))
            dsf = split(pf * (dot(do16, cv, 1, 1) - delta[:16]) * scale)
            dq = dot2(ds, k, 1, 0) * scale
            dq = jnp.concatenate([dq[:16] + dot2(dsf, ck, 1, 0), dq[16:]], axis=0)
            dqz[t, p, :, head] = dq.astype(bf16)
            turned[:HD, :] += dot(q, ds[0], 0, 0) + dot(q, ds[1], 0, 0)
            turned[HD:, :] += dot(do, prs[0], 0, 0) + dot(do, prs[1], 0, 0)
            dcls[:, :HD] += dot2(dsf, q16, 0, 0)
            dcls[:, HD:] += dot2(pfs, do16, 0, 0)

        dkv_acc[at, :HD] = turned[:HD, :].T * scale
        dkv_acc[at, HD:] = turned[HD:, :].T
        if p == own - 1:
            for k in range(1, nc):
                dcls_send(k).start()
        send_chunk(p)
        if p == 0:
            for k in range(1, nt):
                wz_recv(k).wait_recv()
            w_start(w_first)

    mine = dcls[rows_of(c), :]
    for k in range(1, nc):
        o = lax.rem(c + k, nc)
        remote(dclsr.at[o], dclsr.at[o], dcls_s.at[k], dcls_r.at[o], {"cand": o}).wait_recv()
        mine = mine + dclsr[o]
    top = lax.broadcasted_iota(jnp.int32, (8, 2 * HD), 0)
    for p in range(own):
        at = slice(p * length, p * length + 8)
        dkv_acc[at, :] = dkv_acc[at, :] + jnp.where(top == 0, mine[p : p + 1], 0.0)
    dkvz[t] = dkv_acc[...].astype(bf16)
    send_chunk(own)
    def x_terms(h, weight, start):
        @pl.loop(0, nd)
        def _(i):
            wi = weight(i)
            at = pl.ds(pl.multiple_of(i * nc * part, 128), nc * part)
            for p in range(own):
                rs = slice(p * length, (p + 1) * length)
                v = dot(dqz[h, p], wi[:, :heads], 1, 1)
                v = v + dot(dkvz[h, rs, :], wi[:, heads:], 1, 1)
                if start:
                    gx_acc[rs, at] = v
                else:
                    gx_acc[rs, at] += v

    def q_terms(x, dq):
        v = dot(x[:length], dq(0), 0, 0)
        for p in range(1, own):
            v = v + dot(x[p * length : (p + 1) * length], dq(p), 0, 0)
        return v

    wide = nc * part
    x_terms(t, lambda i: w[pl.ds(pl.multiple_of(t * xcols + i * wide, 16), wide), :], True)
    x = tok[:, block(e_add)]
    gsq[...] = q_terms(x, lambda p: dqz[t, p])
    gsk[...] = dot(x, dkvz[t], 0, 0)
    x = tok[:, block(e)]
    gw_acc[:, :heads] = q_terms(x, lambda p: dqz[t, p])
    gw_acc[:, heads:] = dot(x, dkvz[t], 0, 0)

    def z_pass(n, dist):
        for side in (0, 1):
            src, to = t + dist * (2 * side - 1), t - 2 * side + 1

            @pl.when((src >= 0) & (src < nt))
            def _():
                z_copy(n, src, t, zf_s.at[n, dist, side]).wait_recv()
                if dist < nt - 1:

                    @pl.when((to >= 0) & (to < nt))
                    def _():
                        z_copy(n, src, to, zf_s.at[n, dist, side]).start()

    for n in range(own + 1):
        z_pass(n, 1)
    w_wait((e_gather, e_add))
    w_start(w_second)

    def g_send(half):
        src, dst = (gsk, grk) if half else (gsq, grq)
        return remote(src, dst, g_s.at[half], g_r.at[half], add)

    tok_wait(1)
    for n in range(own):
        p_wait(n)

    @pl.loop(0, 3)
    def _(k):
        gsq[...] += q_terms(tokg[1, k], lambda p: dqp[k, p])

    g_send(0).start()
    p_wait(own)

    @pl.loop(0, 3)
    def _(k):
        gsk[...] += dot(tokg[1, k], dkvp[k], 0, 0)

    g_send(1).start()

    for dist in range(2, nt - 1):
        for n in range(own + 1):
            z_pass(n, dist)
    w_wait((e_far,))
    w_start(w_third)
    tok_wait(0)

    @pl.loop(0, 3)
    def _(k):
        gw_acc[:, :heads] += q_terms(tokg[0, k], lambda p: dqp[k, p])
        gw_acc[:, heads:] += dot(tokg[0, k], dkvp[k], 0, 0)

    w_wait([j * nd + 2 * i + flip for j in range(nc) for i in range(nd // 2)])
    for dist in range(1, nt):
        if dist == nt - 1:
            for n in range(own + 1):
                z_pass(n, dist)
        for side in (0, 1):
            src = t + dist * (2 * side - 1)

            @pl.when((src >= 0) & (src < nt))
            def _():
                x_terms(
                    src,
                    lambda i: wg[src, pl.ds(i * nc, nc)].reshape(wide, heads + 2 * HD),
                    False,
                )

    gx[...] = gx_acc[...].astype(bf16)

    g_send(0).wait_recv()
    g_send(1).wait_recv()
    chunks = (heads + 2 * HD) // 128
    for i in range(chunks):
        if i * 128 < heads:
            v = grq[:, i * 128 : (i + 1) * 128]
        else:
            v = grk[:, i * 128 - heads : (i + 1) * 128 - heads]
        gw[pl.ds(i, cols, stride=chunks), :] = v + gw_acc[:, i * 128 : (i + 1) * 128]

    for k in range(1, nt):
        wz_send(k).wait_send()
    for step in (0, 1):
        for k in range(3):
            tok_send(step, k).wait_send()
    for k in range(1, nc):
        cls_send(k).wait_send()
        dcls_send(k).wait_send()
    for i in range(1, nt):
        h = lax.rem(t + i, nt)
        for k, j, dev in w_first + w_second + w_third:
            wp(k, j, h, dev).wait_send()
    for n in range(own + 1):
        for side in (0, 1):
            to = t + 2 * side - 1

            @pl.when((to >= 0) & (to < nt))
            def _():
                z_copy(n, t, to, z_s.at[n, side]).wait_send()

            for dist in range(1, nt - 1):
                src, on = t + dist * (2 * side - 1), t - 2 * side + 1

                @pl.when((src >= 0) & (src < nt) & (on >= 0) & (on < nt))
                def _():
                    z_copy(n, src, on, zf_s.at[n, dist, side]).wait_send()

        for k in range(3):
            p_send(n, k).wait_send()
    g_send(0).wait_send()
    g_send(1).wait_send()


def fused(sizes, tokens, qkv_weight, lengths, grad_out):
    nc, nt, nd, own, length = sizes
    width, rows = tokens.shape[-1], own * length
    cols, xcols = width // (nc * nd), width // nt
    kv, heads = 2 * HD, GQ * HD
    dma = pltpu.SemaphoreType.DMA
    vmem = pl.BlockSpec(memory_space=pltpu.VMEM)
    flops = 6 * rows * width * (heads + kv)
    attended, grad_x, grad_w = pl.pallas_call(
        functools.partial(kernel, sizes),
        out_shape=(
            jax.ShapeDtypeStruct((rows, heads), bf16),
            jax.ShapeDtypeStruct((rows, xcols), bf16),
            jax.ShapeDtypeStruct((cols * (heads + kv) // 128, 128), f32),
        ),
        in_specs=[vmem, vmem, pl.BlockSpec(memory_space=pltpu.SMEM), vmem],
        out_specs=(vmem, vmem, vmem),
        scratch_shapes=[
            pltpu.VMEM((rows, heads), bf16),
            pltpu.VMEM((rows, kv), bf16),
            pltpu.VMEM((128, kv), bf16),
            pltpu.VMEM((128, kv), f32),
            pltpu.VMEM((nc, 16, kv), f32),
            pltpu.VMEM((rows, kv), f32),
            pltpu.VMEM((kv, length), f32),
            pltpu.VMEM((rows, xcols), f32),
            pltpu.VMEM((2, 3, rows, cols), bf16),
            pltpu.VMEM((nt, nc * nd, xcols // (nc * nd), heads + kv), bf16),
            pltpu.VMEM((nt, own, length, heads), bf16),
            pltpu.VMEM((nt, rows, kv), bf16),
            pltpu.VMEM((3, own, length, heads), bf16),
            pltpu.VMEM((3, rows, kv), bf16),
            pltpu.VMEM((cols, heads), f32),
            pltpu.VMEM((cols, kv), f32),
            pltpu.VMEM((cols, heads), f32),
            pltpu.VMEM((cols, kv), f32),
            pltpu.VMEM((cols, heads + kv), f32),
            dma((nc,)),
            dma((nc,)),
            dma((nc,)),
            dma((nc,)),
            dma((2, 3)),
            dma((2, 3)),
            dma((nt,)),
            dma((nt,)),
            dma((7, nt)),
            dma((nc * nd, nt)),
            dma((own + 1, 2)),
            dma((own + 1, nt)),
            dma((own + 1, nt, 2)),
            dma((own + 1, 3)),
            dma((own + 1, 3)),
            dma((2,)),
            dma((2,)),
        ],
        compiler_params=pltpu.CompilerParams(
            collective_id=0, has_side_effects=True, vmem_limit_bytes=58 * 2**20
        ),
        cost_estimate=pl.CostEstimate(
            flops=flops, bytes_accessed=16 * 2**20, transcendentals=rows * length * GQ
        ),
    )(
        tokens.reshape(rows, width),
        qkv_weight.reshape(width, heads + kv),
        lengths.reshape(own),
        grad_out.reshape(rows, heads),
    )
    return (
        attended.reshape(1, own, length, 1, heads),
        grad_x.reshape(1, own, length, xcols),
        grad_w.reshape(cols, 1, heads + kv),
    )


def local(sizes, tokens, qkv_weight, lengths, grad_out):
    nc, nt, nd = sizes
    lists, own, length, width = tokens.shape
    ne = nc * nd
    fits = (
        lists == 1
        and qkv_weight.shape[1] == 1
        and nd == 4
        and nc == 2
        and nt >= 3
        and own <= 8
        and width % (ne * 128) == 0
        and width % (ne * nt * 128) == 0
        and length % 128 == 0
        and 2 * ne * own * length * (width // ne) <= 6 * 2**20
    )
    if fits:
        return fused((nc, nt, nd, own, length), tokens, qkv_weight, lengths, grad_out)
    return body(tokens, qkv_weight, lengths, grad_out)


def solution(mesh):
    placed = (
        P("dp", "cand", None, None),
        P(None, "tp", None),
        P("dp", "cand"),
        P("dp", "cand", None, "tp", None),
    )
    sizes = tuple(mesh.shape[name] for name in ("cand", "tp", "dp"))
    return jax.shard_map(
        functools.partial(local, sizes),
        mesh=mesh,
        in_specs=placed,
        out_specs=(
            P("dp", "cand", None, "tp", None),
            P("dp", "cand", None, "tp"),
            P(("cand", "dp"), "tp", None),
        ),
        check_vma=False,
    )
```

```python
import functools
import math

import jax
import jax.numpy as jnp
from jax import lax
from jax.experimental import pallas as pl
from jax.experimental.pallas import tpu as pltpu
from jax.sharding import PartitionSpec as P

GQ = 4
HD = 128


highest = lax.Precision.HIGHEST
masked_value = -1e30


def attend(queries, key_rows, value_rows, cls_keys, cls_values, lengths, first_index):
    head_size = queries.shape[-1]
    factor = 1.0 / math.sqrt(head_size)
    cand_total = queries.shape[0]
    seq_len = queries.shape[1]
    listed = cls_keys.shape[0]
    scores = jnp.einsum("clhge,cmhe->chglm", queries, key_rows, precision=highest) * factor
    visible = jnp.arange(seq_len)[None, :] < lengths[:, None]
    scores = jnp.where(visible[:, None, None, None, :], scores, masked_value)
    row_peak = lax.stop_gradient(jnp.max(scores, axis=-1, keepdims=True))
    weights = jnp.exp(scores - row_peak)
    totals = jnp.sum(weights, axis=-1)
    blended = jnp.einsum("chglm,cmhe->clhge", weights, value_rows, precision=highest)
    blended = blended / jnp.transpose(totals, (0, 3, 1, 2))[..., None]
    across = jnp.einsum("chge,ahe->chga", queries[:, 0], cls_keys, precision=highest) * factor
    own_slot = jnp.arange(listed)[None, :] == (first_index + jnp.arange(cand_total))[:, None]
    across = jnp.where(own_slot[:, None, None, :], masked_value, across)
    first_row = scores[:, :, :, 0, :]
    joint_peak = lax.stop_gradient(
        jnp.maximum(jnp.max(first_row, axis=-1), jnp.max(across, axis=-1))
    )[..., None]
    local_weights = jnp.exp(first_row - joint_peak)
    far_weights = jnp.exp(across - joint_peak)
    denominator = jnp.sum(local_weights, axis=-1) + jnp.sum(far_weights, axis=-1)
    head_row = jnp.einsum("chgm,cmhe->chge", local_weights, value_rows, precision=highest)
    head_row = head_row + jnp.einsum("chga,ahe->chge", far_weights, cls_values, precision=highest)
    head_row = head_row / denominator[..., None]
    return blended.at[:, 0].set(head_row)


def body(tokens, qkv_weight, lengths, grad_out):
    list_count, cand_count, seq_len, model_width = tokens.shape
    local_heads = qkv_weight.shape[1]
    row_count = list_count * cand_count * seq_len
    flat_rows = tokens.reshape(row_count, model_width)
    weight_mat = qkv_weight.reshape(model_width, -1)
    packed = jnp.dot(flat_rows, weight_mat, preferred_element_type=jnp.float32).astype(jnp.bfloat16)
    packed = packed.reshape(list_count, cand_count, seq_len, local_heads, (GQ + 2) * HD)
    query_part = packed[..., : GQ * HD].reshape(
        list_count, cand_count, seq_len, local_heads, GQ, HD
    )
    key_part = packed[..., GQ * HD : (GQ + 1) * HD]
    value_part = packed[..., (GQ + 1) * HD :]
    cls_keys, cls_values = (
        lax.all_gather(key_part[:, :, 0], "cand", axis=1, tiled=True),
        lax.all_gather(value_part[:, :, 0], "cand", axis=1, tiled=True),
    )
    first_index = lax.axis_index("cand") * cand_count

    def forward(q_in, k_in, v_in, ck_in, cv_in):
        return jax.vmap(attend, in_axes=(0, 0, 0, 0, 0, 0, None))(
            q_in, k_in, v_in, ck_in, cv_in, lengths, first_index
        )

    result, pullback = jax.vjp(
        forward,
        query_part.astype(jnp.float32),
        key_part.astype(jnp.float32),
        value_part.astype(jnp.float32),
        cls_keys.astype(jnp.float32),
        cls_values.astype(jnp.float32),
    )
    attended = result.reshape(list_count, cand_count, seq_len, local_heads, GQ * HD).astype(
        jnp.bfloat16
    )
    upstream = grad_out.astype(jnp.float32).reshape(
        list_count, cand_count, seq_len, local_heads, GQ, HD
    )
    d_query, d_key, d_value, d_cls_key, d_cls_value = pullback(upstream)
    own_key, own_value = (
        lax.psum_scatter(d_cls_key, "cand", scatter_dimension=1, tiled=True),
        lax.psum_scatter(d_cls_value, "cand", scatter_dimension=1, tiled=True),
    )
    d_key = d_key.at[:, :, 0].add(own_key)
    d_value = d_value.at[:, :, 0].add(own_value)
    d_packed = jnp.concatenate(
        [d_query.reshape(list_count, cand_count, seq_len, local_heads, GQ * HD), d_key, d_value],
        axis=-1,
    )
    d_packed = d_packed.astype(jnp.bfloat16).reshape(row_count, -1)
    partial_x = lax.dot_general(
        d_packed, weight_mat, (((1,), (1,)), ((), ())), preferred_element_type=jnp.float32
    )
    grad_x = lax.psum_scatter(partial_x, "tp", scatter_dimension=1, tiled=True).astype(jnp.bfloat16)
    grad_x = grad_x.reshape(list_count, cand_count, seq_len, -1)
    grad_w = lax.psum_scatter(
        lax.dot_general(
            flat_rows, d_packed, (((0,), (0,)), ((), ())), preferred_element_type=jnp.float32
        ),
        ("cand", "dp"),
        scatter_dimension=0,
        tiled=True,
    )
    return (attended, grad_x, grad_w.reshape(grad_w.shape[0], local_heads, -1))


MESH = pl.DeviceIdType.MESH
f32 = jnp.float32
bf16 = jnp.bfloat16


def dot(a, b, ca, cb):
    return lax.dot_general(a, b, (((ca,), (cb,)), ((), ())), preferred_element_type=f32)


def split(x):
    hi = x.astype(bf16)
    return hi, (x - hi.astype(f32)).astype(bf16)


def dot2(x, b, ca, cb):
    return dot(x[0], b, ca, cb) + dot(x[1], b, ca, cb)


def kernel(
    sizes,
    tok_h,
    w_h,
    lens,
    go_h,
    att,
    gx,
    gw,
    tok,
    w,
    go,
    ld,
    qb,
    kvb,
    cls,
    dcls,
    dclsr,
    dkv_acc,
    turned,
    gx_acc,
    tokg,
    wg,
    dqz,
    dkvz,
    dqp,
    dkvp,
    gsq,
    gsk,
    grq,
    grk,
    gw_acc,
    cls_s,
    cls_r,
    dcls_s,
    dcls_r,
    tok_s,
    tok_r,
    wz_s,
    wz_r,
    wp_s,
    wp_r,
    z_s,
    z_r,
    zf_s,
    p_s,
    p_r,
    g_s,
    g_r,
):
    nc, nt, nd, own, length = sizes
    c, t, d = lax.axis_index("cand"), lax.axis_index("tp"), lax.axis_index("dp")
    y, core = d // 2, lax.rem(d, 2)
    cols = tok.shape[1] // (nc * nd)
    xcols = w.shape[0] // nt
    part = xcols // (nc * nd)
    heads = GQ * HD
    scale = 1.0 / math.sqrt(HD)

    kv_cols, q_cols = pl.ds(heads, 2 * HD), pl.ds(0, heads)
    loads = [
        pltpu.make_async_copy(a, b, ld.at[i])
        for i, (a, b) in enumerate(
            (
                (w_h.at[:, kv_cols], w.at[:, kv_cols]),
                (tok_h, tok),
                (w_h.at[:, q_cols], w.at[:, q_cols]),
                (go_h, go),
            )
        )
    ]
    for load in loads:
        load.start()

    cls[...] = jnp.zeros_like(cls)
    dcls[...] = jnp.zeros_like(dcls)

    def at_x(kk):
        return {"cand": 1 - c, "dp": 2 * y + kk}

    def at_y(kk):
        return {"cand": c, "dp": 2 * (1 - y) + kk}

    def index(dev):
        return dev["cand"] * nd + dev["dp"]

    flip = 1 - core
    sib = {"cand": c, "dp": 2 * y + flip}
    gather = {"cand": c * core + (1 - c) * flip, "dp": 2 * (y * flip + (1 - y) * core) + core}
    add = {"cand": c * flip + (1 - c) * core, "dp": 2 * (y * core + (1 - y) * flip) + core}
    e, e_sib, e_gather, e_add = c * nd + d, index(sib), index(gather), index(add)
    e_far = (1 - c) * nd + 2 * (1 - y) + core
    sib_add = (c * core + (1 - c) * flip) * nd + 2 * (y * flip + (1 - y) * core) + flip
    users = (
        (sib, 0, (e_sib, sib_add)),
        (at_x(0), 1 + core, (index(at_x(0)), (1 - c) * nd + 2 * (1 - y))),
        (at_y(1), 1 + core, (index(at_y(1)), (1 - c) * nd + 2 * (1 - y) + 1)),
    )

    barrier = pltpu.get_barrier_semaphore()
    for dev in (sib, at_x(0), at_x(1), at_y(0), at_y(1)):
        pl.semaphore_signal(barrier, inc=1, device_id=dev, device_id_type=MESH)
    for k in range(1, nt):
        pl.semaphore_signal(
            barrier, inc=1, device_id={"tp": lax.rem(t + k, nt)}, device_id_type=MESH
        )
    pl.semaphore_wait(barrier, 5 + nt - 1)

    def remote(src, dst, ss, rs, dev):
        return pltpu.make_async_remote_copy(
            src_ref=src, dst_ref=dst, send_sem=ss, recv_sem=rs, device_id=dev, device_id_type=MESH
        )

    def wz_send(k):
        o = lax.rem(t + k, nt)
        return remote(
            w_h.at[pl.ds(pl.multiple_of(o * xcols + e * part, 16), part)],
            wg.at[t, e],
            wz_s.at[k],
            wz_r.at[t],
            {"tp": o},
        )

    def wz_recv(k):
        h = lax.rem(t + k, nt)
        return remote(wg.at[h, e], wg.at[h, e], wz_s.at[k], wz_r.at[h], {"tp": h})

    def wp(k, j, h, dev):
        return remote(wg.at[h, j], wg.at[h, j], wp_s.at[k, h], wp_r.at[j, h], dev)

    w_first = ((0, e, at_x(core)), (1, e, at_y(core)), (2, e, sib))
    w_second = ((3, e_gather, add), (4, e_gather, sib), (5, e_add, sib))
    w_third = ((6, e_far, sib),)

    def w_start(copies):
        for i in range(1, nt):
            for k, j, dev in copies:
                wp(k, j, lax.rem(t + i, nt), dev).start()

    def w_wait(slots):
        for i in range(1, nt):
            for j in slots:
                wp(0, j, lax.rem(t + i, nt), sib).wait_recv()

    def block(j):
        return pl.ds(pl.multiple_of(j * cols, 128), cols)

    def tok_send(step, k):
        dev, slot, blocks = users[k]
        return remote(
            tok_h.at[:, block(blocks[step])],
            tokg.at[step, slot],
            tok_s.at[step, k],
            tok_r.at[step, slot],
            dev,
        )

    def tok_wait(step):
        for k in range(3):
            remote(
                tokg.at[step, k], tokg.at[step, k], tok_s.at[step, k], tok_r.at[step, k], sib
            ).wait_recv()

    for k in range(1, nt):
        wz_send(k).start()
    for step in (1, 0):
        for k in range(3):
            tok_send(step, k).start()

    def zbuf(n, s):
        return dqz.at[s, n] if n < own else dkvz.at[s]

    def pbuf(n, s):
        return dqp.at[s, n] if n < own else dkvp.at[s]

    def z_copy(n, s, to, ss):
        return remote(zbuf(n, s), zbuf(n, s), ss, z_r.at[n, s], {"tp": to})

    def p_send(n, k):
        dev, slot, _ = users[k]
        return remote(zbuf(n, t), pbuf(n, slot), p_s.at[n, k], p_r.at[n, slot], dev)

    def p_wait(n):
        for k in range(3):
            remote(pbuf(n, k), pbuf(n, k), p_s.at[n, k], p_r.at[n, k], sib).wait_recv()

    def send_chunk(n):
        for side in (0, 1):
            to = t + 2 * side - 1

            @pl.when((to >= 0) & (to < nt))
            def _():
                z_copy(n, t, to, z_s.at[n, side]).start()

        for k in range(3):
            p_send(n, k).start()

    def z_pass(n, dist):
        for side in (0, 1):
            src, to = t + dist * (2 * side - 1), t - 2 * side + 1

            @pl.when((src >= 0) & (src < nt))
            def _():
                z_copy(n, src, t, zf_s.at[n, dist, side]).wait_recv()
                if dist < nt - 1:

                    @pl.when((to >= 0) & (to < nt))
                    def _():
                        z_copy(n, src, to, zf_s.at[n, dist, side]).start()

    loads[0].wait()
    loads[1].wait()
    kvb[...] = dot(tok[...], w[:, heads:], 1, 0).astype(bf16)
    first = lax.broadcasted_iota(jnp.int32, (16, 2 * HD), 0)
    mine = jnp.zeros((16, 2 * HD), f32)
    for p in range(own):
        cls_row = kvb[p * length : p * length + 16, :].astype(f32)[0:1]
        mine = jnp.where(first == p, cls_row, mine)

    def rows_of(j):
        return pl.ds(pl.multiple_of(j * 16, 16), 16)

    cls[rows_of(c), :] = mine.astype(bf16)

    def cls_send(k):
        return remote(
            cls.at[rows_of(c)], cls.at[rows_of(c)], cls_s.at[k], cls_r.at[c], {"cand": lax.rem(c + k, nc)}
        )

    def cls_recv(k):
        o = lax.rem(c + k, nc)
        return remote(cls.at[rows_of(o)], cls.at[rows_of(o)], cls_s.at[k], cls_r.at[o], {"cand": o})

    def dcls_send(k):
        o = lax.rem(c + k, nc)
        return remote(dcls.at[rows_of(o)], dclsr.at[c], dcls_s.at[k], dcls_r.at[c], {"cand": o})

    for k in range(1, nc):
        cls_send(k).start()

    loads[2].wait()

    @pl.loop(0, heads // 256)
    def _(i):
        at = pl.ds(pl.multiple_of(i * 256, 256), 256)
        qb[:, at] = dot(tok[...], w[:, at], 1, 0).astype(bf16)

    for k in range(1, nc):
        cls_recv(k).wait_recv()

    loads[3].wait()
    far_lane = lax.broadcasted_iota(jnp.int32, (16, 128), 1)
    far_row = lax.broadcasted_iota(jnp.int32, (16, 128), 0)
    lane = lax.broadcasted_iota(jnp.int32, (length, length), 1)

    for p in range(own):
        at = slice(p * length, (p + 1) * length)
        visible = lane < lens[p]
        listed = (far_row == 0) & (lax.rem(far_lane, 16) < own) & (far_lane < nc * 16)
        listed = listed & (far_lane != c * 16 + p)

        turned[...] = jnp.zeros_like(turned)

        @pl.loop(0, GQ, unroll=2)
        def _(g):
            head = pl.ds(pl.multiple_of(g * HD, HD), HD)
            q, do = qb[at, head], go[at, head]
            k, v = kvb[at, :HD], kvb[at, HD:]
            ck, cv = cls[:, :HD], cls[:, HD:]
            q16, do16 = q[:16], do[:16]
            s = jnp.where(visible, dot(q, k, 1, 1), masked_value)
            f = jnp.where(listed, dot(q16, ck, 1, 1), masked_value)
            m = jnp.max(s, axis=1, keepdims=True)
            m16 = jnp.maximum(m[:16], jnp.max(f, axis=1, keepdims=True))
            m = jnp.concatenate([m16, m[16:]], axis=0)
            pr, pf = jnp.exp((s - m) * scale), jnp.exp((f - m16) * scale)
            total = jnp.sum(pr, axis=1, keepdims=True)
            t16 = total[:16] + jnp.sum(pf, axis=1, keepdims=True)
            total = jnp.concatenate([t16, total[16:]], axis=0)
            over = 1.0 / total
            pr, pf = pr * over, pf * over[:16]
            prs, pfs = split(pr), split(pf)
            o = dot2(prs, v, 1, 0)
            o = jnp.concatenate([o[:16] + dot2(pfs, cv, 1, 0), o[16:]], axis=0)
            att[at, head] = o.astype(bf16)
            delta = jnp.sum(o * do.astype(f32), axis=1, keepdims=True)
            ds = split(pr * (dot(do, v, 1, 1) - delta))
            dsf = split(pf * (dot(do16, cv, 1, 1) - delta[:16]) * scale)
            dq = dot2(ds, k, 1, 0) * scale
            dq = jnp.concatenate([dq[:16] + dot2(dsf, ck, 1, 0), dq[16:]], axis=0)
            dqz[t, p, :, head] = dq.astype(bf16)
            turned[:HD, :] += dot(q, ds[0], 0, 0) + dot(q, ds[1], 0, 0)
            turned[HD:, :] += dot(do, prs[0], 0, 0) + dot(do, prs[1], 0, 0)
            dcls[:, :HD] += dot2(dsf, q16, 0, 0)
            dcls[:, HD:] += dot2(pfs, do16, 0, 0)

        dkv_acc[at, :HD] = turned[:HD, :].T * scale
        dkv_acc[at, HD:] = turned[HD:, :].T
        if p == own - 1:
            for k in range(1, nc):
                dcls_send(k).start()
        send_chunk(p)
        if p == 0:
            for k in range(1, nt):
                wz_recv(k).wait_recv()
            w_start(w_first)
        if p > 0:
            z_pass(p - 1, 1)

    mine = dcls[rows_of(c), :]
    for k in range(1, nc):
        o = lax.rem(c + k, nc)
        remote(dclsr.at[o], dclsr.at[o], dcls_s.at[k], dcls_r.at[o], {"cand": o}).wait_recv()
        mine = mine + dclsr[o]
    top = lax.broadcasted_iota(jnp.int32, (8, 2 * HD), 0)
    for p in range(own):
        at = slice(p * length, p * length + 8)
        dkv_acc[at, :] = dkv_acc[at, :] + jnp.where(top == 0, mine[p : p + 1], 0.0)
    dkvz[t] = dkv_acc[...].astype(bf16)
    send_chunk(own)
    def x_terms(h, weight, start):
        @pl.loop(0, nd)
        def _(i):
            wi = weight(i)
            at = pl.ds(pl.multiple_of(i * nc * part, 128), nc * part)
            for p in range(own):
                rs = slice(p * length, (p + 1) * length)
                v = dot(dqz[h, p], wi[:, :heads], 1, 1)
                v = v + dot(dkvz[h, rs, :], wi[:, heads:], 1, 1)
                if start:
                    gx_acc[rs, at] = v
                else:
                    gx_acc[rs, at] += v

    def q_terms(x, dq):
        v = dot(x[:length], dq(0), 0, 0)
        for p in range(1, own):
            v = v + dot(x[p * length : (p + 1) * length], dq(p), 0, 0)
        return v

    wide = nc * part
    x_terms(t, lambda i: w[pl.ds(pl.multiple_of(t * xcols + i * wide, 16), wide), :], True)
    z_pass(own - 1, 1)
    x = tok[:, block(e_add)]
    gsq[...] = q_terms(x, lambda p: dqz[t, p])
    gsk[...] = dot(x, dkvz[t], 0, 0)
    x = tok[:, block(e)]
    gw_acc[:, :heads] = q_terms(x, lambda p: dqz[t, p])
    gw_acc[:, heads:] = dot(x, dkvz[t], 0, 0)

    z_pass(own, 1)
    for dist in range(2, nt - 1):
        for n in range(own):
            z_pass(n, dist)
    w_wait((e_gather, e_add))
    w_start(w_second)

    def g_send(half):
        src, dst = (gsk, grk) if half else (gsq, grq)
        return remote(src, dst, g_s.at[half], g_r.at[half], add)

    tok_wait(1)
    for n in range(own):
        p_wait(n)

    @pl.loop(0, 3)
    def _(k):
        gsq[...] += q_terms(tokg[1, k], lambda p: dqp[k, p])

    g_send(0).start()
    for dist in range(2, nt - 1):
        z_pass(own, dist)
    p_wait(own)

    @pl.loop(0, 3)
    def _(k):
        gsk[...] += dot(tokg[1, k], dkvp[k], 0, 0)

    g_send(1).start()

    w_wait((e_far,))
    w_start(w_third)
    tok_wait(0)

    @pl.loop(0, 3)
    def _(k):
        gw_acc[:, :heads] += q_terms(tokg[0, k], lambda p: dqp[k, p])
        gw_acc[:, heads:] += dot(tokg[0, k], dkvp[k], 0, 0)

    w_wait([j * nd + 2 * i + flip for j in range(nc) for i in range(nd // 2)])
    for dist in range(1, nt):
        if dist == nt - 1:
            for n in range(own + 1):
                z_pass(n, dist)
        for side in (0, 1):
            src = t + dist * (2 * side - 1)

            @pl.when((src >= 0) & (src < nt))
            def _():
                x_terms(
                    src,
                    lambda i: wg[src, pl.ds(i * nc, nc)].reshape(wide, heads + 2 * HD),
                    False,
                )

    gx[...] = gx_acc[...].astype(bf16)

    g_send(0).wait_recv()
    g_send(1).wait_recv()
    chunks = (heads + 2 * HD) // 128
    for i in range(chunks):
        if i * 128 < heads:
            v = grq[:, i * 128 : (i + 1) * 128]
        else:
            v = grk[:, i * 128 - heads : (i + 1) * 128 - heads]
        gw[pl.ds(i, cols, stride=chunks), :] = v + gw_acc[:, i * 128 : (i + 1) * 128]

    for k in range(1, nt):
        wz_send(k).wait_send()
    for step in (0, 1):
        for k in range(3):
            tok_send(step, k).wait_send()
    for k in range(1, nc):
        cls_send(k).wait_send()
        dcls_send(k).wait_send()
    for i in range(1, nt):
        h = lax.rem(t + i, nt)
        for k, j, dev in w_first + w_second + w_third:
            wp(k, j, h, dev).wait_send()
    for n in range(own + 1):
        for side in (0, 1):
            to = t + 2 * side - 1

            @pl.when((to >= 0) & (to < nt))
            def _():
                z_copy(n, t, to, z_s.at[n, side]).wait_send()

            for dist in range(1, nt - 1):
                src, on = t + dist * (2 * side - 1), t - 2 * side + 1

                @pl.when((src >= 0) & (src < nt) & (on >= 0) & (on < nt))
                def _():
                    z_copy(n, src, on, zf_s.at[n, dist, side]).wait_send()

        for k in range(3):
            p_send(n, k).wait_send()
    g_send(0).wait_send()
    g_send(1).wait_send()


PIECES = 4


def publish(a, b, c, a_out, b_out, c_out, sem):
    copies = []
    for i, (src, dst) in enumerate(((a, a_out), (b, b_out), (c, c_out))):
        rows = src.shape[0] // PIECES
        for j in range(PIECES):
            at = pl.ds(j * rows, rows)
            copies.append(pltpu.make_async_copy(src.at[at], dst.at[at], sem.at[i, j]))
    for copy in copies:
        copy.start()
    for copy in copies:
        copy.wait()


def fused(sizes, tokens, qkv_weight, lengths, grad_out):
    nc, nt, nd, own, length = sizes
    width, rows = tokens.shape[-1], own * length
    cols, xcols = width // (nc * nd), width // nt
    kv, heads = 2 * HD, GQ * HD
    dma = pltpu.SemaphoreType.DMA
    vmem, hbm = pl.BlockSpec(memory_space=pltpu.VMEM), pl.BlockSpec(memory_space=pl.ANY)
    flops = 6 * rows * width * (heads + kv)
    attended, grad_x, grad_w = pl.pallas_call(
        functools.partial(kernel, sizes),
        out_shape=(
            jax.ShapeDtypeStruct((rows, heads), bf16),
            jax.ShapeDtypeStruct((rows, xcols), bf16),
            jax.ShapeDtypeStruct((cols * (heads + kv) // 128, 128), f32),
        ),
        in_specs=[hbm, hbm, pl.BlockSpec(memory_space=pltpu.SMEM), hbm],
        out_specs=(vmem, vmem, vmem),
        scratch_shapes=[
            pltpu.VMEM((rows, width), bf16),
            pltpu.VMEM((width, heads + kv), bf16),
            pltpu.VMEM((rows, heads), bf16),
            dma((4,)),
            pltpu.VMEM((rows, heads), bf16),
            pltpu.VMEM((rows, kv), bf16),
            pltpu.VMEM((128, kv), bf16),
            pltpu.VMEM((128, kv), f32),
            pltpu.VMEM((nc, 16, kv), f32),
            pltpu.VMEM((rows, kv), f32),
            pltpu.VMEM((kv, length), f32),
            pltpu.VMEM((rows, xcols), f32),
            pltpu.VMEM((2, 3, rows, cols), bf16),
            pltpu.VMEM((nt, nc * nd, xcols // (nc * nd), heads + kv), bf16),
            pltpu.VMEM((nt, own, length, heads), bf16),
            pltpu.VMEM((nt, rows, kv), bf16),
            pltpu.VMEM((3, own, length, heads), bf16),
            pltpu.VMEM((3, rows, kv), bf16),
            pltpu.VMEM((cols, heads), f32),
            pltpu.VMEM((cols, kv), f32),
            pltpu.VMEM((cols, heads), f32),
            pltpu.VMEM((cols, kv), f32),
            pltpu.VMEM((cols, heads + kv), f32),
            dma((nc,)),
            dma((nc,)),
            dma((nc,)),
            dma((nc,)),
            dma((2, 3)),
            dma((2, 3)),
            dma((nt,)),
            dma((nt,)),
            dma((7, nt)),
            dma((nc * nd, nt)),
            dma((own + 1, 2)),
            dma((own + 1, nt)),
            dma((own + 1, nt, 2)),
            dma((own + 1, 3)),
            dma((own + 1, 3)),
            dma((2,)),
            dma((2,)),
        ],
        compiler_params=pltpu.CompilerParams(
            collective_id=0, has_side_effects=True, vmem_limit_bytes=58 * 2**20
        ),
        cost_estimate=pl.CostEstimate(
            flops=flops, bytes_accessed=16 * 2**20, transcendentals=rows * length * GQ
        ),
    )(
        tokens.reshape(rows, width),
        qkv_weight.reshape(width, heads + kv),
        lengths.reshape(own),
        grad_out.reshape(rows, heads),
    )
    results = (attended, grad_x, grad_w)
    attended, grad_x, grad_w = pl.pallas_call(
        publish,
        out_shape=tuple(jax.ShapeDtypeStruct(a.shape, a.dtype) for a in results),
        in_specs=[hbm] * 3,
        out_specs=(hbm,) * 3,
        scratch_shapes=[dma((3, PIECES))],
        compiler_params=pltpu.CompilerParams(vmem_limit_bytes=62 * 2**20),
    )(*results)
    return (
        attended.reshape(1, own, length, 1, heads),
        grad_x.reshape(1, own, length, xcols),
        grad_w.reshape(cols, 1, heads + kv),
    )


def local(sizes, tokens, qkv_weight, lengths, grad_out):
    nc, nt, nd = sizes
    lists, own, length, width = tokens.shape
    ne = nc * nd
    fits = (
        lists == 1
        and qkv_weight.shape[1] == 1
        and nd == 4
        and nc == 2
        and nt >= 3
        and own <= 8
        and width % (ne * 128) == 0
        and width % (ne * nt * 128) == 0
        and length % 128 == 0
        and 2 * ne * own * length * (width // ne) <= 6 * 2**20
    )
    if fits:
        return fused((nc, nt, nd, own, length), tokens, qkv_weight, lengths, grad_out)
    return body(tokens, qkv_weight, lengths, grad_out)


def solution(mesh):
    placed = (
        P("dp", "cand", None, None),
        P(None, "tp", None),
        P("dp", "cand"),
        P("dp", "cand", None, "tp", None),
    )
    sizes = tuple(mesh.shape[name] for name in ("cand", "tp", "dp"))
    return jax.shard_map(
        functools.partial(local, sizes),
        mesh=mesh,
        in_specs=placed,
        out_specs=(
            P("dp", "cand", None, "tp", None),
            P("dp", "cand", None, "tp"),
            P(("cand", "dp"), "tp", None),
        ),
        check_vma=False,
    )
```

```python
import functools
import math

import jax
import jax.numpy as jnp
from jax import lax
from jax.experimental import pallas as pl
from jax.experimental.pallas import tpu as pltpu
from jax.sharding import PartitionSpec as P

GQ = 4
HD = 128


highest = lax.Precision.HIGHEST
masked_value = -1e30


def attend(queries, key_rows, value_rows, cls_keys, cls_values, lengths, first_index):
    head_size = queries.shape[-1]
    factor = 1.0 / math.sqrt(head_size)
    cand_total = queries.shape[0]
    seq_len = queries.shape[1]
    listed = cls_keys.shape[0]
    scores = jnp.einsum("clhge,cmhe->chglm", queries, key_rows, precision=highest) * factor
    visible = jnp.arange(seq_len)[None, :] < lengths[:, None]
    scores = jnp.where(visible[:, None, None, None, :], scores, masked_value)
    row_peak = lax.stop_gradient(jnp.max(scores, axis=-1, keepdims=True))
    weights = jnp.exp(scores - row_peak)
    totals = jnp.sum(weights, axis=-1)
    blended = jnp.einsum("chglm,cmhe->clhge", weights, value_rows, precision=highest)
    blended = blended / jnp.transpose(totals, (0, 3, 1, 2))[..., None]
    across = jnp.einsum("chge,ahe->chga", queries[:, 0], cls_keys, precision=highest) * factor
    own_slot = jnp.arange(listed)[None, :] == (first_index + jnp.arange(cand_total))[:, None]
    across = jnp.where(own_slot[:, None, None, :], masked_value, across)
    first_row = scores[:, :, :, 0, :]
    joint_peak = lax.stop_gradient(
        jnp.maximum(jnp.max(first_row, axis=-1), jnp.max(across, axis=-1))
    )[..., None]
    local_weights = jnp.exp(first_row - joint_peak)
    far_weights = jnp.exp(across - joint_peak)
    denominator = jnp.sum(local_weights, axis=-1) + jnp.sum(far_weights, axis=-1)
    head_row = jnp.einsum("chgm,cmhe->chge", local_weights, value_rows, precision=highest)
    head_row = head_row + jnp.einsum("chga,ahe->chge", far_weights, cls_values, precision=highest)
    head_row = head_row / denominator[..., None]
    return blended.at[:, 0].set(head_row)


def body(tokens, qkv_weight, lengths, grad_out):
    list_count, cand_count, seq_len, model_width = tokens.shape
    local_heads = qkv_weight.shape[1]
    row_count = list_count * cand_count * seq_len
    flat_rows = tokens.reshape(row_count, model_width)
    weight_mat = qkv_weight.reshape(model_width, -1)
    packed = jnp.dot(flat_rows, weight_mat, preferred_element_type=jnp.float32).astype(jnp.bfloat16)
    packed = packed.reshape(list_count, cand_count, seq_len, local_heads, (GQ + 2) * HD)
    query_part = packed[..., : GQ * HD].reshape(
        list_count, cand_count, seq_len, local_heads, GQ, HD
    )
    key_part = packed[..., GQ * HD : (GQ + 1) * HD]
    value_part = packed[..., (GQ + 1) * HD :]
    cls_keys, cls_values = (
        lax.all_gather(key_part[:, :, 0], "cand", axis=1, tiled=True),
        lax.all_gather(value_part[:, :, 0], "cand", axis=1, tiled=True),
    )
    first_index = lax.axis_index("cand") * cand_count

    def forward(q_in, k_in, v_in, ck_in, cv_in):
        return jax.vmap(attend, in_axes=(0, 0, 0, 0, 0, 0, None))(
            q_in, k_in, v_in, ck_in, cv_in, lengths, first_index
        )

    result, pullback = jax.vjp(
        forward,
        query_part.astype(jnp.float32),
        key_part.astype(jnp.float32),
        value_part.astype(jnp.float32),
        cls_keys.astype(jnp.float32),
        cls_values.astype(jnp.float32),
    )
    attended = result.reshape(list_count, cand_count, seq_len, local_heads, GQ * HD).astype(
        jnp.bfloat16
    )
    upstream = grad_out.astype(jnp.float32).reshape(
        list_count, cand_count, seq_len, local_heads, GQ, HD
    )
    d_query, d_key, d_value, d_cls_key, d_cls_value = pullback(upstream)
    own_key, own_value = (
        lax.psum_scatter(d_cls_key, "cand", scatter_dimension=1, tiled=True),
        lax.psum_scatter(d_cls_value, "cand", scatter_dimension=1, tiled=True),
    )
    d_key = d_key.at[:, :, 0].add(own_key)
    d_value = d_value.at[:, :, 0].add(own_value)
    d_packed = jnp.concatenate(
        [d_query.reshape(list_count, cand_count, seq_len, local_heads, GQ * HD), d_key, d_value],
        axis=-1,
    )
    d_packed = d_packed.astype(jnp.bfloat16).reshape(row_count, -1)
    partial_x = lax.dot_general(
        d_packed, weight_mat, (((1,), (1,)), ((), ())), preferred_element_type=jnp.float32
    )
    grad_x = lax.psum_scatter(partial_x, "tp", scatter_dimension=1, tiled=True).astype(jnp.bfloat16)
    grad_x = grad_x.reshape(list_count, cand_count, seq_len, -1)
    grad_w = lax.psum_scatter(
        lax.dot_general(
            flat_rows, d_packed, (((0,), (0,)), ((), ())), preferred_element_type=jnp.float32
        ),
        ("cand", "dp"),
        scatter_dimension=0,
        tiled=True,
    )
    return (attended, grad_x, grad_w.reshape(grad_w.shape[0], local_heads, -1))


MESH = pl.DeviceIdType.MESH
f32 = jnp.float32
bf16 = jnp.bfloat16


def dot(a, b, ca, cb):
    return lax.dot_general(a, b, (((ca,), (cb,)), ((), ())), preferred_element_type=f32)


def split(x):
    hi = x.astype(bf16)
    return hi, (x - hi.astype(f32)).astype(bf16)


def dot2(x, b, ca, cb):
    return dot(x[0], b, ca, cb) + dot(x[1], b, ca, cb)


def kernel(
    sizes,
    tok_h,
    w_h,
    lens,
    go_h,
    att,
    gx,
    gw,
    tok,
    w,
    go,
    ld,
    qb,
    kvb,
    cls,
    dcls,
    dclsr,
    dkv_acc,
    turned,
    gx_acc,
    tokg,
    wg,
    dqz,
    dkvz,
    dqp,
    dkvp,
    gsq,
    gsk,
    grq,
    grk,
    gw_acc,
    cls_s,
    cls_r,
    dcls_s,
    dcls_r,
    tok_s,
    tok_r,
    wz_s,
    wz_r,
    wp_s,
    wp_r,
    z_s,
    z_r,
    zf_s,
    p_s,
    p_r,
    g_s,
    g_r,
):
    nc, nt, nd, own, length = sizes
    c, t, d = lax.axis_index("cand"), lax.axis_index("tp"), lax.axis_index("dp")
    y, core = d // 2, lax.rem(d, 2)
    cols = tok.shape[1] // (nc * nd)
    xcols = w.shape[0] // nt
    part = xcols // (nc * nd)
    heads = GQ * HD
    scale = 1.0 / math.sqrt(HD)

    kv_cols, q_cols = pl.ds(heads, 2 * HD), pl.ds(0, heads)
    loads = [
        pltpu.make_async_copy(a, b, ld.at[i])
        for i, (a, b) in enumerate(
            (
                (w_h.at[:, kv_cols], w.at[:, kv_cols]),
                (tok_h, tok),
                (w_h.at[:, q_cols], w.at[:, q_cols]),
                (go_h, go),
            )
        )
    ]
    for load in loads:
        load.start()

    cls[...] = jnp.zeros_like(cls)
    dcls[...] = jnp.zeros_like(dcls)

    def at_x(kk):
        return {"cand": 1 - c, "dp": 2 * y + kk}

    def at_y(kk):
        return {"cand": c, "dp": 2 * (1 - y) + kk}

    def index(dev):
        return dev["cand"] * nd + dev["dp"]

    flip = 1 - core
    sib = {"cand": c, "dp": 2 * y + flip}
    gather = {"cand": c * core + (1 - c) * flip, "dp": 2 * (y * flip + (1 - y) * core) + core}
    add = {"cand": c * flip + (1 - c) * core, "dp": 2 * (y * core + (1 - y) * flip) + core}
    e, e_sib, e_gather, e_add = c * nd + d, index(sib), index(gather), index(add)
    e_far = (1 - c) * nd + 2 * (1 - y) + core
    sib_add = (c * core + (1 - c) * flip) * nd + 2 * (y * flip + (1 - y) * core) + flip
    users = (
        (sib, 0, (e_sib, sib_add)),
        (at_x(0), 1 + core, (index(at_x(0)), (1 - c) * nd + 2 * (1 - y))),
        (at_y(1), 1 + core, (index(at_y(1)), (1 - c) * nd + 2 * (1 - y) + 1)),
    )

    barrier = pltpu.get_barrier_semaphore()
    for dev in (sib, at_x(0), at_x(1), at_y(0), at_y(1)):
        pl.semaphore_signal(barrier, inc=1, device_id=dev, device_id_type=MESH)
    for k in range(1, nt):
        pl.semaphore_signal(
            barrier, inc=1, device_id={"tp": lax.rem(t + k, nt)}, device_id_type=MESH
        )
    pl.semaphore_wait(barrier, 5 + nt - 1)

    def remote(src, dst, ss, rs, dev):
        return pltpu.make_async_remote_copy(
            src_ref=src, dst_ref=dst, send_sem=ss, recv_sem=rs, device_id=dev, device_id_type=MESH
        )

    def wz_send(k):
        o = lax.rem(t + k, nt)
        return remote(
            w_h.at[pl.ds(pl.multiple_of(o * xcols + e * part, 16), part)],
            wg.at[t, e],
            wz_s.at[k],
            wz_r.at[t],
            {"tp": o},
        )

    def wz_recv(k):
        h = lax.rem(t + k, nt)
        return remote(wg.at[h, e], wg.at[h, e], wz_s.at[k], wz_r.at[h], {"tp": h})

    def wp(k, j, h, dev):
        return remote(wg.at[h, j], wg.at[h, j], wp_s.at[k, h], wp_r.at[j, h], dev)

    w_first = ((0, e, at_x(core)), (1, e, at_y(core)), (2, e, sib))
    w_second = ((3, e_gather, add), (4, e_gather, sib), (5, e_add, sib))
    w_third = ((6, e_far, sib),)

    def w_start(copies):
        for i in range(1, nt):
            for k, j, dev in copies:
                wp(k, j, lax.rem(t + i, nt), dev).start()

    def w_wait(slots):
        for i in range(1, nt):
            for j in slots:
                wp(0, j, lax.rem(t + i, nt), sib).wait_recv()

    def block(j):
        return pl.ds(pl.multiple_of(j * cols, 128), cols)

    def tok_send(step, k):
        dev, slot, blocks = users[k]
        return remote(
            tok_h.at[:, block(blocks[step])],
            tokg.at[step, slot],
            tok_s.at[step, k],
            tok_r.at[step, slot],
            dev,
        )

    def tok_wait(step):
        for k in range(3):
            remote(
                tokg.at[step, k], tokg.at[step, k], tok_s.at[step, k], tok_r.at[step, k], sib
            ).wait_recv()

    for k in range(1, nt):
        wz_send(k).start()
    for step in (1, 0):
        for k in range(3):
            tok_send(step, k).start()

    def zbuf(n, s):
        return dqz.at[s, n] if n < own else dkvz.at[s]

    def pbuf(n, s):
        return dqp.at[s, n] if n < own else dkvp.at[s]

    def z_copy(n, s, to, ss):
        return remote(zbuf(n, s), zbuf(n, s), ss, z_r.at[n, s], {"tp": to})

    def p_send(n, k):
        dev, slot, _ = users[k]
        return remote(zbuf(n, t), pbuf(n, slot), p_s.at[n, k], p_r.at[n, slot], dev)

    def p_wait(n):
        for k in range(3):
            remote(pbuf(n, k), pbuf(n, k), p_s.at[n, k], p_r.at[n, k], sib).wait_recv()

    def send_chunk(n):
        for side in (0, 1):
            to = t + 2 * side - 1

            @pl.when((to >= 0) & (to < nt))
            def _():
                z_copy(n, t, to, z_s.at[n, side]).start()

        for k in range(3):
            p_send(n, k).start()

    def z_pass(n, dist):
        for side in (0, 1):
            src, to = t + dist * (2 * side - 1), t - 2 * side + 1

            @pl.when((src >= 0) & (src < nt))
            def _():
                z_copy(n, src, t, zf_s.at[n, dist, side]).wait_recv()
                if dist < nt - 1:

                    @pl.when((to >= 0) & (to < nt))
                    def _():
                        z_copy(n, src, to, zf_s.at[n, dist, side]).start()

    loads[0].wait()
    loads[1].wait()
    kvb[...] = dot(tok[...], w[:, heads:], 1, 0).astype(bf16)
    first = lax.broadcasted_iota(jnp.int32, (16, 2 * HD), 0)
    mine = jnp.zeros((16, 2 * HD), f32)
    for p in range(own):
        cls_row = kvb[p * length : p * length + 16, :].astype(f32)[0:1]
        mine = jnp.where(first == p, cls_row, mine)

    def rows_of(j):
        return pl.ds(pl.multiple_of(j * 16, 16), 16)

    cls[rows_of(c), :] = mine.astype(bf16)

    def cls_send(k):
        return remote(
            cls.at[rows_of(c)], cls.at[rows_of(c)], cls_s.at[k], cls_r.at[c], {"cand": lax.rem(c + k, nc)}
        )

    def cls_recv(k):
        o = lax.rem(c + k, nc)
        return remote(cls.at[rows_of(o)], cls.at[rows_of(o)], cls_s.at[k], cls_r.at[o], {"cand": o})

    def dcls_send(k):
        o = lax.rem(c + k, nc)
        return remote(dcls.at[rows_of(o)], dclsr.at[c], dcls_s.at[k], dcls_r.at[c], {"cand": o})

    for k in range(1, nc):
        cls_send(k).start()

    loads[2].wait()
    loads[3].wait()
    far_lane = lax.broadcasted_iota(jnp.int32, (16, 128), 1)
    far_row = lax.broadcasted_iota(jnp.int32, (16, 128), 0)
    lane = lax.broadcasted_iota(jnp.int32, (length, length), 1)

    for p in range(own):
        at = slice(p * length, (p + 1) * length)
        visible = lane < lens[p]
        listed = (far_row == 0) & (lax.rem(far_lane, 16) < own) & (far_lane < nc * 16)
        listed = listed & (far_lane != c * 16 + p)

        turned[...] = jnp.zeros_like(turned)

        @pl.loop(0, heads // 256)
        def _(i):
            to = pl.ds(pl.multiple_of(i * 256, 256), 256)
            qb[at, to] = dot(tok[at, :], w[:, to], 1, 0).astype(bf16)

        if p == 0:
            for k in range(1, nc):
                cls_recv(k).wait_recv()

        def one_head(g):
            head = pl.ds(pl.multiple_of(g * HD, HD), HD)
            q, do = qb[at, head], go[at, head]
            k, v = kvb[at, :HD], kvb[at, HD:]
            ck, cv = cls[:, :HD], cls[:, HD:]
            q16, do16 = q[:16], do[:16]
            s = jnp.where(visible, dot(q, k, 1, 1), masked_value)
            f = jnp.where(listed, dot(q16, ck, 1, 1), masked_value)
            m = jnp.max(s, axis=1, keepdims=True)
            m16 = jnp.maximum(m[:16], jnp.max(f, axis=1, keepdims=True))
            m = jnp.concatenate([m16, m[16:]], axis=0)
            pr, pf = jnp.exp((s - m) * scale), jnp.exp((f - m16) * scale)
            total = jnp.sum(pr, axis=1, keepdims=True)
            t16 = total[:16] + jnp.sum(pf, axis=1, keepdims=True)
            total = jnp.concatenate([t16, total[16:]], axis=0)
            over = 1.0 / total
            pr, pf = pr * over, pf * over[:16]
            prs, pfs = split(pr), split(pf)
            o = dot2(prs, v, 1, 0)
            o = jnp.concatenate([o[:16] + dot2(pfs, cv, 1, 0), o[16:]], axis=0)
            att[at, head] = o.astype(bf16)
            delta = jnp.sum(o * do.astype(f32), axis=1, keepdims=True)
            ds = split(pr * (dot(do, v, 1, 1) - delta))
            dsf = split(pf * (dot(do16, cv, 1, 1) - delta[:16]) * scale)
            dq = dot2(ds, k, 1, 0) * scale
            dq = jnp.concatenate([dq[:16] + dot2(dsf, ck, 1, 0), dq[16:]], axis=0)
            dqz[t, p, :, head] = dq.astype(bf16)
            turned[:HD, :] += dot(q, ds[0], 0, 0) + dot(q, ds[1], 0, 0)
            turned[HD:, :] += dot(do, prs[0], 0, 0) + dot(do, prs[1], 0, 0)
            dcls[:, :HD] += dot2(dsf, q16, 0, 0)
            dcls[:, HD:] += dot2(pfs, do16, 0, 0)

        if p < own - 1:
            pl.loop(0, GQ, unroll=2)(one_head)
        else:
            pl.loop(0, GQ // 2, unroll=2)(one_head)
            for k in range(1, nt):
                wz_recv(k).wait_recv()
            w_start(w_first)
            pl.loop(GQ // 2, GQ, unroll=2)(one_head)
        dkv_acc[at, :HD] = turned[:HD, :].T * scale
        dkv_acc[at, HD:] = turned[HD:, :].T
        if p == own - 1:
            for k in range(1, nc):
                dcls_send(k).start()
        send_chunk(p)
        if p > 0:
            z_pass(p - 1, 1)

    mine = dcls[rows_of(c), :]
    for k in range(1, nc):
        o = lax.rem(c + k, nc)
        remote(dclsr.at[o], dclsr.at[o], dcls_s.at[k], dcls_r.at[o], {"cand": o}).wait_recv()
        mine = mine + dclsr[o]
    top = lax.broadcasted_iota(jnp.int32, (8, 2 * HD), 0)
    for p in range(own):
        at = slice(p * length, p * length + 8)
        dkv_acc[at, :] = dkv_acc[at, :] + jnp.where(top == 0, mine[p : p + 1], 0.0)
    dkvz[t] = dkv_acc[...].astype(bf16)
    send_chunk(own)
    def x_terms(h, weight, start):
        @pl.loop(0, nd)
        def _(i):
            wi = weight(i)
            at = pl.ds(pl.multiple_of(i * nc * part, 128), nc * part)
            for p in range(own):
                rs = slice(p * length, (p + 1) * length)
                v = dot(dqz[h, p], wi[:, :heads], 1, 1)
                v = v + dot(dkvz[h, rs, :], wi[:, heads:], 1, 1)
                if start:
                    gx_acc[rs, at] = v
                else:
                    gx_acc[rs, at] += v

    def q_terms(x, dq):
        v = dot(x[:length], dq(0), 0, 0)
        for p in range(1, own):
            v = v + dot(x[p * length : (p + 1) * length], dq(p), 0, 0)
        return v

    wide = nc * part
    x_terms(t, lambda i: w[pl.ds(pl.multiple_of(t * xcols + i * wide, 16), wide), :], True)
    z_pass(own - 1, 1)
    x = tok[:, block(e_add)]
    gsq[...] = q_terms(x, lambda p: dqz[t, p])
    gsk[...] = dot(x, dkvz[t], 0, 0)
    x = tok[:, block(e)]
    gw_acc[:, :heads] = q_terms(x, lambda p: dqz[t, p])
    gw_acc[:, heads:] = dot(x, dkvz[t], 0, 0)

    z_pass(own, 1)
    for dist in range(2, nt - 1):
        for n in range(own):
            z_pass(n, dist)
    w_wait((e_gather, e_add))
    w_start(w_second)

    def g_send(half):
        src, dst = (gsk, grk) if half else (gsq, grq)
        return remote(src, dst, g_s.at[half], g_r.at[half], add)

    tok_wait(1)
    for n in range(own):
        p_wait(n)

    @pl.loop(0, 3)
    def _(k):
        gsq[...] += q_terms(tokg[1, k], lambda p: dqp[k, p])

    g_send(0).start()
    for dist in range(2, nt - 1):
        z_pass(own, dist)
    p_wait(own)

    @pl.loop(0, 3)
    def _(k):
        gsk[...] += dot(tokg[1, k], dkvp[k], 0, 0)

    g_send(1).start()

    w_wait((e_far,))
    w_start(w_third)
    tok_wait(0)

    @pl.loop(0, 3)
    def _(k):
        gw_acc[:, :heads] += q_terms(tokg[0, k], lambda p: dqp[k, p])
        gw_acc[:, heads:] += dot(tokg[0, k], dkvp[k], 0, 0)

    w_wait([j * nd + 2 * i + flip for j in range(nc) for i in range(nd // 2)])
    for dist in range(1, nt):
        if dist == nt - 1:
            for n in range(own + 1):
                z_pass(n, dist)
        for side in (0, 1):
            src = t + dist * (2 * side - 1)

            @pl.when((src >= 0) & (src < nt))
            def _():
                x_terms(
                    src,
                    lambda i: wg[src, pl.ds(i * nc, nc)].reshape(wide, heads + 2 * HD),
                    False,
                )

    gx[...] = gx_acc[...].astype(bf16)

    g_send(0).wait_recv()
    g_send(1).wait_recv()
    chunks = (heads + 2 * HD) // 128
    for i in range(chunks):
        if i * 128 < heads:
            v = grq[:, i * 128 : (i + 1) * 128]
        else:
            v = grk[:, i * 128 - heads : (i + 1) * 128 - heads]
        gw[pl.ds(i, cols, stride=chunks), :] = v + gw_acc[:, i * 128 : (i + 1) * 128]

    for k in range(1, nt):
        wz_send(k).wait_send()
    for step in (0, 1):
        for k in range(3):
            tok_send(step, k).wait_send()
    for k in range(1, nc):
        cls_send(k).wait_send()
        dcls_send(k).wait_send()
    for i in range(1, nt):
        h = lax.rem(t + i, nt)
        for k, j, dev in w_first + w_second + w_third:
            wp(k, j, h, dev).wait_send()
    for n in range(own + 1):
        for side in (0, 1):
            to = t + 2 * side - 1

            @pl.when((to >= 0) & (to < nt))
            def _():
                z_copy(n, t, to, z_s.at[n, side]).wait_send()

            for dist in range(1, nt - 1):
                src, on = t + dist * (2 * side - 1), t - 2 * side + 1

                @pl.when((src >= 0) & (src < nt) & (on >= 0) & (on < nt))
                def _():
                    z_copy(n, src, on, zf_s.at[n, dist, side]).wait_send()

        for k in range(3):
            p_send(n, k).wait_send()
    g_send(0).wait_send()
    g_send(1).wait_send()


PIECES = 4


def publish(a, b, c, a_out, b_out, c_out, a_mid, b_mid, c_mid, sem_in, sem_out):
    moves = []
    for i, (src, mid, dst) in enumerate(
        ((a, a_mid, a_out), (b, b_mid, b_out), (c, c_mid, c_out))
    ):
        rows = src.shape[0] // PIECES
        for j in range(PIECES):
            at = pl.ds(j * rows, rows)
            moves.append(
                (
                    pltpu.make_async_copy(src.at[at], mid.at[at], sem_in.at[i, j]),
                    pltpu.make_async_copy(mid.at[at], dst.at[at], sem_out.at[i, j]),
                )
            )
    for load, _ in moves:
        load.start()
    for load, store in moves:
        load.wait()
        store.start()
    for _, store in moves:
        store.wait()


def fused(sizes, tokens, qkv_weight, lengths, grad_out):
    nc, nt, nd, own, length = sizes
    width, rows = tokens.shape[-1], own * length
    cols, xcols = width // (nc * nd), width // nt
    kv, heads = 2 * HD, GQ * HD
    dma = pltpu.SemaphoreType.DMA
    vmem, hbm = pl.BlockSpec(memory_space=pltpu.VMEM), pl.BlockSpec(memory_space=pl.ANY)
    flops = 6 * rows * width * (heads + kv)
    attended, grad_x, grad_w = pl.pallas_call(
        functools.partial(kernel, sizes),
        out_shape=(
            jax.ShapeDtypeStruct((rows, heads), bf16),
            jax.ShapeDtypeStruct((rows, xcols), bf16),
            jax.ShapeDtypeStruct((cols * (heads + kv) // 128, 128), f32),
        ),
        in_specs=[hbm, hbm, pl.BlockSpec(memory_space=pltpu.SMEM), hbm],
        out_specs=(vmem, vmem, vmem),
        scratch_shapes=[
            pltpu.VMEM((rows, width), bf16),
            pltpu.VMEM((width, heads + kv), bf16),
            pltpu.VMEM((rows, heads), bf16),
            dma((4,)),
            pltpu.VMEM((rows, heads), bf16),
            pltpu.VMEM((rows, kv), bf16),
            pltpu.VMEM((128, kv), bf16),
            pltpu.VMEM((128, kv), f32),
            pltpu.VMEM((nc, 16, kv), f32),
            pltpu.VMEM((rows, kv), f32),
            pltpu.VMEM((kv, length), f32),
            pltpu.VMEM((rows, xcols), f32),
            pltpu.VMEM((2, 3, rows, cols), bf16),
            pltpu.VMEM((nt, nc * nd, xcols // (nc * nd), heads + kv), bf16),
            pltpu.VMEM((nt, own, length, heads), bf16),
            pltpu.VMEM((nt, rows, kv), bf16),
            pltpu.VMEM((3, own, length, heads), bf16),
            pltpu.VMEM((3, rows, kv), bf16),
            pltpu.VMEM((cols, heads), f32),
            pltpu.VMEM((cols, kv), f32),
            pltpu.VMEM((cols, heads), f32),
            pltpu.VMEM((cols, kv), f32),
            pltpu.VMEM((cols, heads + kv), f32),
            dma((nc,)),
            dma((nc,)),
            dma((nc,)),
            dma((nc,)),
            dma((2, 3)),
            dma((2, 3)),
            dma((nt,)),
            dma((nt,)),
            dma((7, nt)),
            dma((nc * nd, nt)),
            dma((own + 1, 2)),
            dma((own + 1, nt)),
            dma((own + 1, nt, 2)),
            dma((own + 1, 3)),
            dma((own + 1, 3)),
            dma((2,)),
            dma((2,)),
        ],
        compiler_params=pltpu.CompilerParams(
            collective_id=0, has_side_effects=True, vmem_limit_bytes=58 * 2**20
        ),
        cost_estimate=pl.CostEstimate(
            flops=flops, bytes_accessed=16 * 2**20, transcendentals=rows * length * GQ
        ),
    )(
        tokens.reshape(rows, width),
        qkv_weight.reshape(width, heads + kv),
        lengths.reshape(own),
        grad_out.reshape(rows, heads),
    )
    results = (attended, grad_x, grad_w)
    attended, grad_x, grad_w = pl.pallas_call(
        publish,
        out_shape=tuple(jax.ShapeDtypeStruct(a.shape, a.dtype) for a in results),
        in_specs=[hbm] * 3,
        out_specs=(hbm,) * 3,
        scratch_shapes=[pltpu.VMEM(a.shape, a.dtype) for a in results]
        + [dma((3, PIECES)), dma((3, PIECES))],
        compiler_params=pltpu.CompilerParams(vmem_limit_bytes=62 * 2**20),
    )(*results)
    return (
        attended.reshape(1, own, length, 1, heads),
        grad_x.reshape(1, own, length, xcols),
        grad_w.reshape(cols, 1, heads + kv),
    )


def local(sizes, tokens, qkv_weight, lengths, grad_out):
    nc, nt, nd = sizes
    lists, own, length, width = tokens.shape
    ne = nc * nd
    fits = (
        lists == 1
        and qkv_weight.shape[1] == 1
        and nd == 4
        and nc == 2
        and nt >= 3
        and own <= 8
        and width % (ne * 128) == 0
        and width % (ne * nt * 128) == 0
        and length % 128 == 0
        and 2 * ne * own * length * (width // ne) <= 6 * 2**20
    )
    if fits:
        return fused((nc, nt, nd, own, length), tokens, qkv_weight, lengths, grad_out)
    return body(tokens, qkv_weight, lengths, grad_out)


def solution(mesh):
    placed = (
        P("dp", "cand", None, None),
        P(None, "tp", None),
        P("dp", "cand"),
        P("dp", "cand", None, "tp", None),
    )
    sizes = tuple(mesh.shape[name] for name in ("cand", "tp", "dp"))
    return jax.shard_map(
        functools.partial(local, sizes),
        mesh=mesh,
        in_specs=placed,
        out_specs=(
            P("dp", "cand", None, "tp", None),
            P("dp", "cand", None, "tp"),
            P(("cand", "dp"), "tp", None),
        ),
        check_vma=False,
    )
```

```python
import functools
import math

import jax
import jax.numpy as jnp
from jax import lax
from jax.experimental import pallas as pl
from jax.experimental.pallas import tpu as pltpu
from jax.sharding import PartitionSpec as P

GQ = 4
HD = 128


highest = lax.Precision.HIGHEST
masked_value = -1e30


def attend(queries, key_rows, value_rows, cls_keys, cls_values, lengths, first_index):
    head_size = queries.shape[-1]
    factor = 1.0 / math.sqrt(head_size)
    cand_total = queries.shape[0]
    seq_len = queries.shape[1]
    listed = cls_keys.shape[0]
    scores = jnp.einsum("clhge,cmhe->chglm", queries, key_rows, precision=highest) * factor
    visible = jnp.arange(seq_len)[None, :] < lengths[:, None]
    scores = jnp.where(visible[:, None, None, None, :], scores, masked_value)
    row_peak = lax.stop_gradient(jnp.max(scores, axis=-1, keepdims=True))
    weights = jnp.exp(scores - row_peak)
    totals = jnp.sum(weights, axis=-1)
    blended = jnp.einsum("chglm,cmhe->clhge", weights, value_rows, precision=highest)
    blended = blended / jnp.transpose(totals, (0, 3, 1, 2))[..., None]
    across = jnp.einsum("chge,ahe->chga", queries[:, 0], cls_keys, precision=highest) * factor
    own_slot = jnp.arange(listed)[None, :] == (first_index + jnp.arange(cand_total))[:, None]
    across = jnp.where(own_slot[:, None, None, :], masked_value, across)
    first_row = scores[:, :, :, 0, :]
    joint_peak = lax.stop_gradient(
        jnp.maximum(jnp.max(first_row, axis=-1), jnp.max(across, axis=-1))
    )[..., None]
    local_weights = jnp.exp(first_row - joint_peak)
    far_weights = jnp.exp(across - joint_peak)
    denominator = jnp.sum(local_weights, axis=-1) + jnp.sum(far_weights, axis=-1)
    head_row = jnp.einsum("chgm,cmhe->chge", local_weights, value_rows, precision=highest)
    head_row = head_row + jnp.einsum("chga,ahe->chge", far_weights, cls_values, precision=highest)
    head_row = head_row / denominator[..., None]
    return blended.at[:, 0].set(head_row)


def body(tokens, qkv_weight, lengths, grad_out):
    list_count, cand_count, seq_len, model_width = tokens.shape
    local_heads = qkv_weight.shape[1]
    row_count = list_count * cand_count * seq_len
    flat_rows = tokens.reshape(row_count, model_width)
    weight_mat = qkv_weight.reshape(model_width, -1)
    packed = jnp.dot(flat_rows, weight_mat, preferred_element_type=jnp.float32).astype(jnp.bfloat16)
    packed = packed.reshape(list_count, cand_count, seq_len, local_heads, (GQ + 2) * HD)
    query_part = packed[..., : GQ * HD].reshape(
        list_count, cand_count, seq_len, local_heads, GQ, HD
    )
    key_part = packed[..., GQ * HD : (GQ + 1) * HD]
    value_part = packed[..., (GQ + 1) * HD :]
    cls_keys, cls_values = (
        lax.all_gather(key_part[:, :, 0], "cand", axis=1, tiled=True),
        lax.all_gather(value_part[:, :, 0], "cand", axis=1, tiled=True),
    )
    first_index = lax.axis_index("cand") * cand_count

    def forward(q_in, k_in, v_in, ck_in, cv_in):
        return jax.vmap(attend, in_axes=(0, 0, 0, 0, 0, 0, None))(
            q_in, k_in, v_in, ck_in, cv_in, lengths, first_index
        )

    result, pullback = jax.vjp(
        forward,
        query_part.astype(jnp.float32),
        key_part.astype(jnp.float32),
        value_part.astype(jnp.float32),
        cls_keys.astype(jnp.float32),
        cls_values.astype(jnp.float32),
    )
    attended = result.reshape(list_count, cand_count, seq_len, local_heads, GQ * HD).astype(
        jnp.bfloat16
    )
    upstream = grad_out.astype(jnp.float32).reshape(
        list_count, cand_count, seq_len, local_heads, GQ, HD
    )
    d_query, d_key, d_value, d_cls_key, d_cls_value = pullback(upstream)
    own_key, own_value = (
        lax.psum_scatter(d_cls_key, "cand", scatter_dimension=1, tiled=True),
        lax.psum_scatter(d_cls_value, "cand", scatter_dimension=1, tiled=True),
    )
    d_key = d_key.at[:, :, 0].add(own_key)
    d_value = d_value.at[:, :, 0].add(own_value)
    d_packed = jnp.concatenate(
        [d_query.reshape(list_count, cand_count, seq_len, local_heads, GQ * HD), d_key, d_value],
        axis=-1,
    )
    d_packed = d_packed.astype(jnp.bfloat16).reshape(row_count, -1)
    partial_x = lax.dot_general(
        d_packed, weight_mat, (((1,), (1,)), ((), ())), preferred_element_type=jnp.float32
    )
    grad_x = lax.psum_scatter(partial_x, "tp", scatter_dimension=1, tiled=True).astype(jnp.bfloat16)
    grad_x = grad_x.reshape(list_count, cand_count, seq_len, -1)
    grad_w = lax.psum_scatter(
        lax.dot_general(
            flat_rows, d_packed, (((0,), (0,)), ((), ())), preferred_element_type=jnp.float32
        ),
        ("cand", "dp"),
        scatter_dimension=0,
        tiled=True,
    )
    return (attended, grad_x, grad_w.reshape(grad_w.shape[0], local_heads, -1))


MESH = pl.DeviceIdType.MESH
f32 = jnp.float32
bf16 = jnp.bfloat16


def dot(a, b, ca, cb):
    return lax.dot_general(a, b, (((ca,), (cb,)), ((), ())), preferred_element_type=f32)


def split(x):
    hi = x.astype(bf16)
    return hi, (x - hi.astype(f32)).astype(bf16)


def dot2(x, b, ca, cb):
    return dot(x[0], b, ca, cb) + dot(x[1], b, ca, cb)


def kernel(
    sizes,
    tok_h,
    w_h,
    lens,
    go_h,
    att,
    gx,
    gw,
    tok,
    w,
    go,
    ld,
    qb,
    kvb,
    cls,
    dcls,
    dclsr,
    dkv_acc,
    turned,
    gx_acc,
    tokg,
    wg,
    dqz,
    dkvz,
    dqp,
    dkvp,
    gsq,
    gsk,
    grq,
    grk,
    gw_acc,
    cls_s,
    cls_r,
    dcls_s,
    dcls_r,
    tok_s,
    tok_r,
    wz_s,
    wz_r,
    wp_s,
    wp_r,
    z_s,
    z_r,
    zf_s,
    p_s,
    p_r,
    g_s,
    g_r,
):
    nc, nt, nd, own, length = sizes
    c, t, d = lax.axis_index("cand"), lax.axis_index("tp"), lax.axis_index("dp")
    y, core = d // 2, lax.rem(d, 2)
    cols = tok.shape[1] // (nc * nd)
    xcols = w.shape[0] // nt
    part = xcols // (nc * nd)
    heads = GQ * HD
    scale = 1.0 / math.sqrt(HD)

    kv_cols, q_cols = pl.ds(heads, 2 * HD), pl.ds(0, heads)
    loads = [
        pltpu.make_async_copy(a, b, ld.at[i])
        for i, (a, b) in enumerate(
            (
                (w_h.at[:, kv_cols], w.at[:, kv_cols]),
                (tok_h, tok),
                (w_h.at[:, q_cols], w.at[:, q_cols]),
                (go_h, go),
            )
        )
    ]
    for load in loads:
        load.start()

    cls[...] = jnp.zeros_like(cls)
    dcls[...] = jnp.zeros_like(dcls)

    def at_x(kk):
        return {"cand": 1 - c, "dp": 2 * y + kk}

    def at_y(kk):
        return {"cand": c, "dp": 2 * (1 - y) + kk}

    def index(dev):
        return dev["cand"] * nd + dev["dp"]

    flip = 1 - core
    sib = {"cand": c, "dp": 2 * y + flip}
    gather = {"cand": c * core + (1 - c) * flip, "dp": 2 * (y * flip + (1 - y) * core) + core}
    add = {"cand": c * flip + (1 - c) * core, "dp": 2 * (y * core + (1 - y) * flip) + core}
    e, e_sib, e_gather, e_add = c * nd + d, index(sib), index(gather), index(add)
    e_far = (1 - c) * nd + 2 * (1 - y) + core
    sib_add = (c * core + (1 - c) * flip) * nd + 2 * (y * flip + (1 - y) * core) + flip
    users = (
        (sib, 0, (e_sib, sib_add)),
        (at_x(0), 1 + core, (index(at_x(0)), (1 - c) * nd + 2 * (1 - y))),
        (at_y(1), 1 + core, (index(at_y(1)), (1 - c) * nd + 2 * (1 - y) + 1)),
    )

    barrier = pltpu.get_barrier_semaphore()
    for dev in (sib, at_x(0), at_x(1), at_y(0), at_y(1)):
        pl.semaphore_signal(barrier, inc=1, device_id=dev, device_id_type=MESH)
    for k in range(1, nt):
        pl.semaphore_signal(
            barrier, inc=1, device_id={"tp": lax.rem(t + k, nt)}, device_id_type=MESH
        )
    pl.semaphore_wait(barrier, 5 + nt - 1)

    def remote(src, dst, ss, rs, dev):
        return pltpu.make_async_remote_copy(
            src_ref=src, dst_ref=dst, send_sem=ss, recv_sem=rs, device_id=dev, device_id_type=MESH
        )

    def wz_send(k):
        o = lax.rem(t + k, nt)
        return remote(
            w_h.at[pl.ds(pl.multiple_of(o * xcols + e * part, 16), part)],
            wg.at[t, e],
            wz_s.at[k],
            wz_r.at[t],
            {"tp": o},
        )

    def wz_recv(k):
        h = lax.rem(t + k, nt)
        return remote(wg.at[h, e], wg.at[h, e], wz_s.at[k], wz_r.at[h], {"tp": h})

    def wp(k, j, h, dev):
        return remote(wg.at[h, j], wg.at[h, j], wp_s.at[k, h], wp_r.at[j, h], dev)

    w_first = ((0, e, at_x(core)), (1, e, at_y(core)), (2, e, sib))
    w_second = ((3, e_gather, add), (4, e_gather, sib), (5, e_add, sib))
    w_third = ((6, e_far, sib),)

    def w_start(copies):
        for i in range(1, nt):
            for k, j, dev in copies:
                wp(k, j, lax.rem(t + i, nt), dev).start()

    def w_wait(slots):
        for i in range(1, nt):
            for j in slots:
                wp(0, j, lax.rem(t + i, nt), sib).wait_recv()

    def block(j):
        return pl.ds(pl.multiple_of(j * cols, 128), cols)

    def tok_send(step, k):
        dev, slot, blocks = users[k]
        return remote(
            tok_h.at[:, block(blocks[step])],
            tokg.at[step, slot],
            tok_s.at[step, k],
            tok_r.at[step, slot],
            dev,
        )

    def tok_wait(step):
        for k in range(3):
            remote(
                tokg.at[step, k], tokg.at[step, k], tok_s.at[step, k], tok_r.at[step, k], sib
            ).wait_recv()

    for k in range(1, nt):
        wz_send(k).start()
    for step in (1, 0):
        for k in range(3):
            tok_send(step, k).start()

    def zbuf(n, s):
        return dqz.at[s, n] if n < own else dkvz.at[s]

    def pbuf(n, s):
        return dqp.at[s, n] if n < own else dkvp.at[s]

    def z_copy(n, s, to, ss):
        return remote(zbuf(n, s), zbuf(n, s), ss, z_r.at[n, s], {"tp": to})

    def p_send(n, k):
        dev, slot, _ = users[k]
        return remote(zbuf(n, t), pbuf(n, slot), p_s.at[n, k], p_r.at[n, slot], dev)

    def p_wait(n):
        for k in range(3):
            remote(pbuf(n, k), pbuf(n, k), p_s.at[n, k], p_r.at[n, k], sib).wait_recv()

    def send_chunk(n):
        for side in (0, 1):
            to = t + 2 * side - 1

            @pl.when((to >= 0) & (to < nt))
            def _():
                z_copy(n, t, to, z_s.at[n, side]).start()

        for k in range(3):
            p_send(n, k).start()

    def z_pass(n, dist):
        for side in (0, 1):
            src, to = t + dist * (2 * side - 1), t - 2 * side + 1

            @pl.when((src >= 0) & (src < nt))
            def _():
                z_copy(n, src, t, zf_s.at[n, dist, side]).wait_recv()
                if dist < nt - 1:

                    @pl.when((to >= 0) & (to < nt))
                    def _():
                        z_copy(n, src, to, zf_s.at[n, dist, side]).start()

    loads[0].wait()
    loads[1].wait()
    kvb[...] = dot(tok[...], w[:, heads:], 1, 0).astype(bf16)
    first = lax.broadcasted_iota(jnp.int32, (16, 2 * HD), 0)
    mine = jnp.zeros((16, 2 * HD), f32)
    for p in range(own):
        cls_row = kvb[p * length : p * length + 16, :].astype(f32)[0:1]
        mine = jnp.where(first == p, cls_row, mine)

    def rows_of(j):
        return pl.ds(pl.multiple_of(j * 16, 16), 16)

    cls[rows_of(c), :] = mine.astype(bf16)

    def cls_send(k):
        return remote(
            cls.at[rows_of(c)], cls.at[rows_of(c)], cls_s.at[k], cls_r.at[c], {"cand": lax.rem(c + k, nc)}
        )

    def cls_recv(k):
        o = lax.rem(c + k, nc)
        return remote(cls.at[rows_of(o)], cls.at[rows_of(o)], cls_s.at[k], cls_r.at[o], {"cand": o})

    def dcls_send(k):
        o = lax.rem(c + k, nc)
        return remote(dcls.at[rows_of(o)], dclsr.at[c], dcls_s.at[k], dcls_r.at[c], {"cand": o})

    for k in range(1, nc):
        cls_send(k).start()

    loads[2].wait()
    loads[3].wait()
    far_lane = lax.broadcasted_iota(jnp.int32, (16, 128), 1)
    far_row = lax.broadcasted_iota(jnp.int32, (16, 128), 0)
    lane = lax.broadcasted_iota(jnp.int32, (length, length), 1)

    for p in range(own):
        at = slice(p * length, (p + 1) * length)
        visible = lane < lens[p]
        listed = (far_row == 0) & (lax.rem(far_lane, 16) < own) & (far_lane < nc * 16)
        listed = listed & (far_lane != c * 16 + p)

        turned[...] = jnp.zeros_like(turned)

        @pl.loop(0, heads // 256)
        def _(i):
            to = pl.ds(pl.multiple_of(i * 256, 256), 256)
            qb[at, to] = dot(tok[at, :], w[:, to], 1, 0).astype(bf16)

        if p == 0:
            for k in range(1, nc):
                cls_recv(k).wait_recv()

        def one_head(g):
            head = pl.ds(pl.multiple_of(g * HD, HD), HD)
            q, do = qb[at, head], go[at, head]
            k, v = kvb[at, :HD], kvb[at, HD:]
            ck, cv = cls[:, :HD], cls[:, HD:]
            q16, do16 = q[:16], do[:16]
            s = jnp.where(visible, dot(q, k, 1, 1), masked_value)
            f = jnp.where(listed, dot(q16, ck, 1, 1), masked_value)
            m = jnp.max(s, axis=1, keepdims=True)
            m16 = jnp.maximum(m[:16], jnp.max(f, axis=1, keepdims=True))
            m = jnp.concatenate([m16, m[16:]], axis=0)
            pr, pf = jnp.exp((s - m) * scale), jnp.exp((f - m16) * scale)
            total = jnp.sum(pr, axis=1, keepdims=True)
            t16 = total[:16] + jnp.sum(pf, axis=1, keepdims=True)
            total = jnp.concatenate([t16, total[16:]], axis=0)
            over = 1.0 / total
            pr, pf = pr * over, pf * over[:16]
            prs, pfs = split(pr), split(pf)
            o = dot2(prs, v, 1, 0)
            o = jnp.concatenate([o[:16] + dot2(pfs, cv, 1, 0), o[16:]], axis=0)
            att[at, head] = o.astype(bf16)
            delta = jnp.sum(o * do.astype(f32), axis=1, keepdims=True)
            ds = split(pr * (dot(do, v, 1, 1) - delta))
            dsf = split(pf * (dot(do16, cv, 1, 1) - delta[:16]) * scale)
            dq = dot2(ds, k, 1, 0) * scale
            dq = jnp.concatenate([dq[:16] + dot2(dsf, ck, 1, 0), dq[16:]], axis=0)
            dqz[t, p, :, head] = dq.astype(bf16)
            turned[:HD, :] += dot(q, ds[0], 0, 0) + dot(q, ds[1], 0, 0)
            turned[HD:, :] += dot(do, prs[0], 0, 0) + dot(do, prs[1], 0, 0)
            dcls[:, :HD] += dot2(dsf, q16, 0, 0)
            dcls[:, HD:] += dot2(pfs, do16, 0, 0)

        if p < own - 1:
            pl.loop(0, GQ, unroll=2)(one_head)
        else:
            pl.loop(0, GQ // 2, unroll=2)(one_head)
            for k in range(1, nt):
                wz_recv(k).wait_recv()
            w_start(w_first)
            pl.loop(GQ // 2, GQ, unroll=2)(one_head)
        dkv_acc[at, :HD] = turned[:HD, :].T * scale
        dkv_acc[at, HD:] = turned[HD:, :].T
        if p == own - 1:
            for k in range(1, nc):
                dcls_send(k).start()
        send_chunk(p)
        if p > 0:
            z_pass(p - 1, 1)

    mine = dcls[rows_of(c), :]
    for k in range(1, nc):
        o = lax.rem(c + k, nc)
        remote(dclsr.at[o], dclsr.at[o], dcls_s.at[k], dcls_r.at[o], {"cand": o}).wait_recv()
        mine = mine + dclsr[o]
    top = lax.broadcasted_iota(jnp.int32, (8, 2 * HD), 0)
    for p in range(own):
        at = slice(p * length, p * length + 8)
        dkv_acc[at, :] = dkv_acc[at, :] + jnp.where(top == 0, mine[p : p + 1], 0.0)
    dkvz[t] = dkv_acc[...].astype(bf16)
    send_chunk(own)
    def x_terms(h, weight, start):
        @pl.loop(0, nd)
        def _(i):
            wi = weight(i)
            at = pl.ds(pl.multiple_of(i * nc * part, 128), nc * part)
            for p in range(own):
                rs = slice(p * length, (p + 1) * length)
                v = dot(dqz[h, p], wi[:, :heads], 1, 1)
                v = v + dot(dkvz[h, rs, :], wi[:, heads:], 1, 1)
                if start:
                    gx_acc[rs, at] = v
                else:
                    gx_acc[rs, at] += v

    def q_terms(x, dq):
        v = dot(x[:length], dq(0), 0, 0)
        for p in range(1, own):
            v = v + dot(x[p * length : (p + 1) * length], dq(p), 0, 0)
        return v

    wide = nc * part
    x_terms(t, lambda i: w[pl.ds(pl.multiple_of(t * xcols + i * wide, 16), wide), :], True)
    z_pass(own - 1, 1)
    x = tok[:, block(e_add)]
    gsq[...] = q_terms(x, lambda p: dqz[t, p])
    gsk[...] = dot(x, dkvz[t], 0, 0)
    x = tok[:, block(e)]
    gw_acc[:, :heads] = q_terms(x, lambda p: dqz[t, p])
    gw_acc[:, heads:] = dot(x, dkvz[t], 0, 0)

    z_pass(own, 1)
    for dist in range(2, nt - 1):
        for n in range(own):
            z_pass(n, dist)

    def g_send(half):
        src, dst = (gsk, grk) if half else (gsq, grq)
        return remote(src, dst, g_s.at[half], g_r.at[half], add)

    tok_wait(1)
    for n in range(own):
        p_wait(n)

    @pl.loop(0, 3)
    def _(k):
        gsq[...] += q_terms(tokg[1, k], lambda p: dqp[k, p])

    g_send(0).start()
    w_wait((e_gather, e_add))
    w_start(w_second)
    for dist in range(2, nt - 1):
        z_pass(own, dist)
    p_wait(own)

    @pl.loop(0, 3)
    def _(k):
        gsk[...] += dot(tokg[1, k], dkvp[k], 0, 0)

    g_send(1).start()

    w_wait((e_far,))
    w_start(w_third)
    tok_wait(0)

    @pl.loop(0, 3)
    def _(k):
        gw_acc[:, :heads] += q_terms(tokg[0, k], lambda p: dqp[k, p])
        gw_acc[:, heads:] += dot(tokg[0, k], dkvp[k], 0, 0)

    w_wait([j * nd + 2 * i + flip for j in range(nc) for i in range(nd // 2)])
    for dist in range(1, nt):
        if dist == nt - 1:
            for n in range(own + 1):
                z_pass(n, dist)
        for side in (0, 1):
            src = t + dist * (2 * side - 1)

            @pl.when((src >= 0) & (src < nt))
            def _():
                x_terms(
                    src,
                    lambda i: wg[src, pl.ds(i * nc, nc)].reshape(wide, heads + 2 * HD),
                    False,
                )

    gx[...] = gx_acc[...].astype(bf16)

    g_send(0).wait_recv()
    g_send(1).wait_recv()
    chunks = (heads + 2 * HD) // 128
    for i in range(chunks):
        if i * 128 < heads:
            v = grq[:, i * 128 : (i + 1) * 128]
        else:
            v = grk[:, i * 128 - heads : (i + 1) * 128 - heads]
        gw[pl.ds(i, cols, stride=chunks), :] = v + gw_acc[:, i * 128 : (i + 1) * 128]

    for k in range(1, nt):
        wz_send(k).wait_send()
    for step in (0, 1):
        for k in range(3):
            tok_send(step, k).wait_send()
    for k in range(1, nc):
        cls_send(k).wait_send()
        dcls_send(k).wait_send()
    for i in range(1, nt):
        h = lax.rem(t + i, nt)
        for k, j, dev in w_first + w_second + w_third:
            wp(k, j, h, dev).wait_send()
    for n in range(own + 1):
        for side in (0, 1):
            to = t + 2 * side - 1

            @pl.when((to >= 0) & (to < nt))
            def _():
                z_copy(n, t, to, z_s.at[n, side]).wait_send()

            for dist in range(1, nt - 1):
                src, on = t + dist * (2 * side - 1), t - 2 * side + 1

                @pl.when((src >= 0) & (src < nt) & (on >= 0) & (on < nt))
                def _():
                    z_copy(n, src, on, zf_s.at[n, dist, side]).wait_send()

        for k in range(3):
            p_send(n, k).wait_send()
    g_send(0).wait_send()
    g_send(1).wait_send()


PIECES = 4


def publish(a, b, c, a_out, b_out, c_out, a_mid, b_mid, c_mid, sem_in, sem_out):
    moves = []
    for i, (src, mid, dst) in enumerate(
        ((a, a_mid, a_out), (b, b_mid, b_out), (c, c_mid, c_out))
    ):
        rows = src.shape[0] // PIECES
        for j in range(PIECES):
            at = pl.ds(j * rows, rows)
            moves.append(
                (
                    pltpu.make_async_copy(src.at[at], mid.at[at], sem_in.at[i, j]),
                    pltpu.make_async_copy(mid.at[at], dst.at[at], sem_out.at[i, j]),
                )
            )
    for load, _ in moves:
        load.start()
    for load, store in moves:
        load.wait()
        store.start()
    for _, store in moves:
        store.wait()


def fused(sizes, tokens, qkv_weight, lengths, grad_out):
    nc, nt, nd, own, length = sizes
    width, rows = tokens.shape[-1], own * length
    cols, xcols = width // (nc * nd), width // nt
    kv, heads = 2 * HD, GQ * HD
    dma = pltpu.SemaphoreType.DMA
    vmem, hbm = pl.BlockSpec(memory_space=pltpu.VMEM), pl.BlockSpec(memory_space=pl.ANY)
    flops = 6 * rows * width * (heads + kv)
    attended, grad_x, grad_w = pl.pallas_call(
        functools.partial(kernel, sizes),
        out_shape=(
            jax.ShapeDtypeStruct((rows, heads), bf16),
            jax.ShapeDtypeStruct((rows, xcols), bf16),
            jax.ShapeDtypeStruct((cols * (heads + kv) // 128, 128), f32),
        ),
        in_specs=[hbm, hbm, pl.BlockSpec(memory_space=pltpu.SMEM), hbm],
        out_specs=(vmem, vmem, vmem),
        scratch_shapes=[
            pltpu.VMEM((rows, width), bf16),
            pltpu.VMEM((width, heads + kv), bf16),
            pltpu.VMEM((rows, heads), bf16),
            dma((4,)),
            pltpu.VMEM((rows, heads), bf16),
            pltpu.VMEM((rows, kv), bf16),
            pltpu.VMEM((128, kv), bf16),
            pltpu.VMEM((128, kv), f32),
            pltpu.VMEM((nc, 16, kv), f32),
            pltpu.VMEM((rows, kv), f32),
            pltpu.VMEM((kv, length), f32),
            pltpu.VMEM((rows, xcols), f32),
            pltpu.VMEM((2, 3, rows, cols), bf16),
            pltpu.VMEM((nt, nc * nd, xcols // (nc * nd), heads + kv), bf16),
            pltpu.VMEM((nt, own, length, heads), bf16),
            pltpu.VMEM((nt, rows, kv), bf16),
            pltpu.VMEM((3, own, length, heads), bf16),
            pltpu.VMEM((3, rows, kv), bf16),
            pltpu.VMEM((cols, heads), f32),
            pltpu.VMEM((cols, kv), f32),
            pltpu.VMEM((cols, heads), f32),
            pltpu.VMEM((cols, kv), f32),
            pltpu.VMEM((cols, heads + kv), f32),
            dma((nc,)),
            dma((nc,)),
            dma((nc,)),
            dma((nc,)),
            dma((2, 3)),
            dma((2, 3)),
            dma((nt,)),
            dma((nt,)),
            dma((7, nt)),
            dma((nc * nd, nt)),
            dma((own + 1, 2)),
            dma((own + 1, nt)),
            dma((own + 1, nt, 2)),
            dma((own + 1, 3)),
            dma((own + 1, 3)),
            dma((2,)),
            dma((2,)),
        ],
        compiler_params=pltpu.CompilerParams(
            collective_id=0, has_side_effects=True, vmem_limit_bytes=58 * 2**20
        ),
        cost_estimate=pl.CostEstimate(
            flops=flops, bytes_accessed=16 * 2**20, transcendentals=rows * length * GQ
        ),
    )(
        tokens.reshape(rows, width),
        qkv_weight.reshape(width, heads + kv),
        lengths.reshape(own),
        grad_out.reshape(rows, heads),
    )
    results = (attended, grad_x, grad_w)
    attended, grad_x, grad_w = pl.pallas_call(
        publish,
        out_shape=tuple(jax.ShapeDtypeStruct(a.shape, a.dtype) for a in results),
        in_specs=[hbm] * 3,
        out_specs=(hbm,) * 3,
        scratch_shapes=[pltpu.VMEM(a.shape, a.dtype) for a in results]
        + [dma((3, PIECES)), dma((3, PIECES))],
        compiler_params=pltpu.CompilerParams(vmem_limit_bytes=62 * 2**20),
    )(*results)
    return (
        attended.reshape(1, own, length, 1, heads),
        grad_x.reshape(1, own, length, xcols),
        grad_w.reshape(cols, 1, heads + kv),
    )


def local(sizes, tokens, qkv_weight, lengths, grad_out):
    nc, nt, nd = sizes
    lists, own, length, width = tokens.shape
    ne = nc * nd
    fits = (
        lists == 1
        and qkv_weight.shape[1] == 1
        and nd == 4
        and nc == 2
        and nt >= 3
        and own <= 8
        and width % (ne * 128) == 0
        and width % (ne * nt * 128) == 0
        and length % 128 == 0
        and 2 * ne * own * length * (width // ne) <= 6 * 2**20
    )
    if fits:
        return fused((nc, nt, nd, own, length), tokens, qkv_weight, lengths, grad_out)
    return body(tokens, qkv_weight, lengths, grad_out)


def solution(mesh):
    placed = (
        P("dp", "cand", None, None),
        P(None, "tp", None),
        P("dp", "cand"),
        P("dp", "cand", None, "tp", None),
    )
    sizes = tuple(mesh.shape[name] for name in ("cand", "tp", "dp"))
    return jax.shard_map(
        functools.partial(local, sizes),
        mesh=mesh,
        in_specs=placed,
        out_specs=(
            P("dp", "cand", None, "tp", None),
            P("dp", "cand", None, "tp"),
            P(("cand", "dp"), "tp", None),
        ),
        check_vma=False,
    )
```
